128 devices in a mesh: dp: 4 (over y), owner: 32 (over x, z, core).
Axes of the slice: x: 4, y: 4, z: 4, core: 2. Of those that a mesh axis runs over, the one named last changes fastest.
Arguments:
- gradient: bfloat16 [128, 2048, 768], P(None, ('dp', 'owner'))
- momentum: float32 [128, 2048, 768], P(None, ('dp', 'owner'))
- owner_table: int32 [128], replicated, may hold values from 0 to 127, as said below
Outputs:
- new_momentum: float32 [128, 2048, 768], P(None, ('dp', 'owner'))
- update: bfloat16 [128, 2048, 768], P(None, ('dp', 'owner'))
- owner_log: float32 [128, 2], P(('dp', 'owner'))
The draws below stay inside these ranges and needn't reach their ends.
Inputs may be any that keep to these rules, and one draw needn't show every extreme that they name: `owner_table`: each device owns at most 2 matrices; in every draw some device owns exactly 2.
All inputs are finite; a program needn't handle non-finite values.
Results may differ from the reference program's by a relative error of at most 0.0076.
Values may be sent and summed in bfloat16 or wider, within the bound.
A program may use at most 128 MiB of HBM per device.

```python
import math
import jax
import jax.numpy as jnp
from jax import lax

D = 2048
FF = 768
CAP = 2
NS_STEPS = 2
MATS = 128


def shared_scales(key, trend):
    row_key, col_key = jax.random.split(key)
    position = jnp.arange(D, dtype=jnp.float32) / (D - 1)
    row_scale = (trend ** position)[None, :, None] * jnp.exp(jax.random.uniform(row_key, (MATS, D, 1), jnp.float32) * math.log(10.0))
    col_scale = jnp.exp(jax.random.uniform(col_key, (MATS, 1, FF), jnp.float32) * math.log(10.0))
    return (row_scale, col_scale)


def draw_gradient(key, part):
    row_scale, col_scale = shared_scales(key, 3.0)
    key = jax.random.fold_in(key, 11)
    noise_key = jax.random.fold_in(key, 0)
    noise = jax.random.normal(noise_key, (MATS, D, FF), jnp.float32)
    return (row_scale * col_scale * noise).astype(jnp.bfloat16)


def draw_momentum(key, part):
    row_scale, col_scale = shared_scales(key, 3.0)
    key = jax.random.fold_in(key, 23)
    noise = jax.random.normal(key, (MATS, D, FF), jnp.float32)
    return (0.5 * row_scale * col_scale * noise).astype(jnp.float32)


def draw_owner_table(key, part):
    key = jax.random.fold_in(key, 37)
    perm_key, count_key = jax.random.split(key)
    shuffled = jax.random.permutation(perm_key, MATS).astype(jnp.int32)
    doubled = jax.random.randint(count_key, (), 1, MATS // 4 + 1).astype(jnp.int32)
    position = jnp.arange(MATS, dtype=jnp.int32)
    shifted = shuffled[jnp.minimum(position + doubled, MATS - 1)]
    return jnp.where(position < doubled, shifted, shuffled).astype(jnp.int32)


def setup_inputs(seed: int = 0) -> dict:
    splits = jax.random.split(jax.random.key(seed), 4)
    return {
        "gradient": draw_gradient(jax.random.fold_in(splits[3], 71), 0),
        "momentum": draw_momentum(jax.random.fold_in(splits[3], 71), 0),
        "owner_table": draw_owner_table(jax.random.fold_in(splits[3], 71), 0),
    }


momentum_decay = 0.95
linear_coef = 3.4445
cubic_coef = -4.775
quintic_coef = 2.0315
norm_epsilon = 1e-07

def newton_schulz(matrix):
    current = matrix
    for repeat in range(NS_STEPS):
        current = lax.optimization_barrier(current)
        gram_mat = lax.dot_general(current, current, (((0,), (0,)), ((), ())), preferred_element_type=jnp.float32).astype(jnp.bfloat16)
        gram_mat = lax.optimization_barrier(gram_mat)
        square = jnp.dot(gram_mat, gram_mat, preferred_element_type=jnp.float32)
        poly_mat = (cubic_coef * gram_mat.astype(jnp.float32) + quintic_coef * square).astype(jnp.bfloat16)
        current = (linear_coef * current.astype(jnp.float32) + jnp.dot(current, poly_mat, preferred_element_type=jnp.float32)).astype(jnp.bfloat16)
    return current

def one_matrix(pair):
    grad_one, moment_one = pair
    grad_float = grad_one.astype(jnp.float32)
    fresh = momentum_decay * moment_one + grad_float
    effective = lax.optimization_barrier((grad_float + momentum_decay * fresh).astype(jnp.bfloat16))
    eff_float = effective.astype(jnp.float32)
    squares = jnp.sum(eff_float * eff_float)
    initial = (eff_float / (jnp.sqrt(squares) + norm_epsilon)).astype(jnp.bfloat16)
    orthogonal = newton_schulz(initial).astype(jnp.float32)
    update = (math.sqrt(D) * orthogonal).astype(jnp.bfloat16)
    rms_value = math.sqrt(D) * jnp.sqrt(jnp.sum(orthogonal * orthogonal) / (D * FF))
    return (fresh, update, rms_value)

def reference(gradient, momentum, owner_table):
    fresh, update, rms_value = lax.map(one_matrix, (gradient, momentum))
    position = jnp.arange(MATS, dtype=jnp.int32)
    same_owner = owner_table[:, None] == owner_table[None, :]
    earlier_one = position[None, :] < position[:, None]
    slot_rank = lax.optimization_barrier(jnp.sum((same_owner & earlier_one).astype(jnp.int32), axis=1)).astype(jnp.int32)
    log_flat = jnp.zeros((MATS * CAP,), jnp.float32).at[owner_table * CAP + slot_rank].set(rms_value)
    return (fresh, update, log_flat.reshape(MATS, CAP))
```

```python
import math

import jax
import jax.numpy as jnp
from jax import lax
from jax.sharding import PartitionSpec as P

CAP = 2
NS_STEPS = 2
AXES = ("dp", "owner")

momentum_decay = 0.95
linear_coef = 3.4445
cubic_coef = -4.775
quintic_coef = 2.0315
norm_epsilon = 1e-07


def orthogonalize(current):
    for repeat in range(NS_STEPS):
        gram_mat = jnp.einsum(
            "df,dg->fg", current, current, preferred_element_type=jnp.float32
        ).astype(jnp.bfloat16)
        square = jnp.dot(gram_mat, gram_mat, preferred_element_type=jnp.float32)
        poly_mat = (cubic_coef * gram_mat.astype(jnp.float32) + quintic_coef * square).astype(
            jnp.bfloat16
        )
        current = (
            linear_coef * current.astype(jnp.float32)
            + jnp.dot(current, poly_mat, preferred_element_type=jnp.float32)
        ).astype(jnp.bfloat16)
    return current


def on_device(gradient, momentum, owner_table):
    matrices, row_count, col_count = gradient.shape
    device_count = lax.axis_size(AXES)
    full_rows = row_count * device_count
    grad_float = gradient.astype(jnp.float32)
    fresh = momentum_decay * momentum + grad_float
    rounded = (grad_float + momentum_decay * fresh).astype(jnp.bfloat16)
    received = lax.all_to_all(rounded, AXES, split_axis=0, concat_axis=0, tiled=True)
    whole = received.reshape(full_rows, col_count).astype(jnp.float32)
    norm = jnp.sqrt(jnp.sum(whole * whole)) + norm_epsilon
    orthogonal = orthogonalize((whole / norm).astype(jnp.bfloat16))
    ortho_float = orthogonal.astype(jnp.float32)
    rms = math.sqrt(full_rows) * jnp.sqrt(
        jnp.sum(ortho_float * ortho_float) / (full_rows * col_count)
    )
    scaled = (math.sqrt(full_rows) * ortho_float).astype(jnp.bfloat16)
    update = lax.all_to_all(
        scaled.reshape(matrices, row_count, col_count), AXES, split_axis=0, concat_axis=0, tiled=True
    )
    every_rms = lax.all_gather(rms, AXES)
    me = lax.axis_index(AXES)
    mine = owner_table == me
    rank = jnp.cumsum(mine.astype(jnp.int32)) - 1
    slots = jnp.arange(CAP, dtype=jnp.int32)
    chosen = mine[None, :] & (rank[None, :] == slots[:, None])
    owner_log = jnp.sum(jnp.where(chosen, every_rms[None, :], 0.0), axis=1)[None, :]
    return (fresh, update, owner_log)


def solution(mesh):
    rows = P(None, AXES, None)
    return jax.shard_map(
        on_device,
        mesh=mesh,
        in_specs=(rows, rows, P()),
        out_specs=(rows, rows, P(AXES, None)),
        check_vma=False,
    )
```

```python
import math

import jax
import jax.numpy as jnp
from jax import lax
from jax.experimental import pallas as pl
from jax.experimental.pallas import tpu as pltpu
from jax.sharding import PartitionSpec as P

AXES = ("dp", "owner")
MESH = pl.DeviceIdType.MESH
F32, BF16 = jnp.float32, jnp.bfloat16
TRANSPOSED = (((0,), (0,)), ((), ()))

momentum_decay = 0.95
linear_coef = 3.4445
cubic_coef = -4.775
quintic_coef = 2.0315
norm_epsilon = 1e-07

DEVICES, CHIPS, CORES = 128, 64, 2
ROWS, FF = 16, 768
TILE = 256
CHUNKS = 4
GROUPS = 8
BLOCKS = 4


def displacement(step):
    n = lax.rem(step * 21, CHIPS)
    return lax.div(n, 16), lax.rem(lax.div(n, 4), 4), lax.rem(n, 4)


def kernel(
    g_hbm, m_hbm, table_ref, fresh_hbm, update_hbm, log_ref,
    gv, mv, rows, sent, gram, poly, total, rms_rows, rms_mine,
    load_sem, fresh_sem, send_sem, recv_sem, own_sem, back_send, back_recv, rms_send, rms_recv,
):
    y, o = lax.axis_index("dp"), lax.axis_index("owner")
    x, z, core = lax.div(o, 8), lax.rem(lax.div(o, 2), 4), lax.rem(o, 2)
    me = y * 32 + o
    sign = 1 - 2 * core

    def chip_at(step, direction):
        dy, dx, dz = displacement(step)
        ty = lax.rem(y + direction * dy + 4, 4)
        tx = lax.rem(x + direction * dx + 4, 4)
        tz = lax.rem(z + direction * dz + 4, 4)
        return ty, tx * 8 + tz * 2

    per = CHIPS // CHUNKS
    loads = []
    for phase in range(CORES):
        for k in range(CHUNKS):
            part = pl.ds(k * per, per)
            pair = (
                pltpu.make_async_copy(
                    g_hbm.at[part, phase], gv.at[part, phase], load_sem.at[0, phase, k]
                ),
                pltpu.make_async_copy(
                    m_hbm.at[part, phase], mv.at[part, phase], load_sem.at[1, phase, k]
                ),
            )
            for copy in pair:
                copy.start()
            loads.append(pair)

    barrier = pltpu.get_barrier_semaphore()

    def greet(i, carry):
        t = lax.rem(me + i, DEVICES)
        pl.semaphore_signal(
            barrier, inc=1, device_id=(lax.div(t, 32), lax.rem(t, 32)), device_id_type=MESH
        )
        return carry

    lax.fori_loop(1, DEVICES, greet, 0)

    def effective(phase):
        for k in range(CHUNKS):
            for copy in loads[phase * CHUNKS + k]:
                copy.wait()

            def one(i, carry):
                grad = gv[i, phase].astype(F32)
                fresh = momentum_decay * mv[i, phase] + grad
                mv[i, phase] = fresh
                gv[i, phase] = (grad + momentum_decay * fresh).astype(BF16)
                return carry

            lax.fori_loop(k * per, (k + 1) * per, one, 0)
            part = pl.ds(k * per, per)
            pltpu.make_async_copy(
                mv.at[part, phase], fresh_hbm.at[part, phase], fresh_sem.at[phase, k]
            ).start()

    def forward(phase):
        mine = y * 16 + x * 4 + z

        @pl.when(core != phase)
        def _():
            pltpu.make_async_remote_copy(
                src_ref=gv.at[mine, phase],
                dst_ref=rows.at[core],
                send_sem=send_sem,
                recv_sem=recv_sem.at[0],
                device_id=(y, x * 8 + z * 2 + phase),
                device_id_type=MESH,
            ).start()

        @pl.when(core == phase)
        def _():
            pltpu.make_async_copy(gv.at[mine, phase], rows.at[core], own_sem.at[0]).start()

        def one(step, carry):
            ty, to = chip_at(step, sign)
            pltpu.make_async_remote_copy(
                src_ref=gv.at[ty * 16 + lax.div(to, 2), phase],
                dst_ref=rows.at[2 * step + core],
                send_sem=send_sem,
                recv_sem=recv_sem.at[lax.div(step, CHIPS // GROUPS)],
                device_id=(ty, to + phase),
                device_id_type=MESH,
            ).start()
            return carry

        lax.fori_loop(1, CHIPS, one, 0)

    effective(0)
    pl.semaphore_wait(barrier, DEVICES - 1)
    forward(0)
    effective(1)
    forward(1)

    size = DEVICES // GROUPS
    total[...] = jnp.zeros_like(total)

    def accumulate(j):
        block = rows[pl.ds(j * size, size)].reshape(size * ROWS, FF)
        flipped = block.T
        for b in range(FF // TILE):
            n = TILE * (b + 1)
            total[0:n, TILE * b : n] += jnp.dot(
                flipped[0:n], block[:, TILE * b : n], preferred_element_type=F32
            )

    pltpu.make_async_copy(rows.at[0], rows.at[0], own_sem.at[0]).wait()
    pltpu.make_async_copy(
        rows.at[pl.ds(0, size - 1)], rows.at[pl.ds(0, size - 1)], recv_sem.at[0]
    ).wait()
    accumulate(0)

    def arrive(j, carry):
        part = rows.at[pl.ds(j * size, size)]
        pltpu.make_async_copy(part, part, recv_sem.at[j]).wait()
        accumulate(j)
        return carry

    lax.fori_loop(1, GROUPS, arrive, 0)

    on_diagonal = lax.broadcasted_iota(jnp.int32, (TILE, TILE), 0) == lax.broadcasted_iota(
        jnp.int32, (TILE, TILE), 1
    )
    squares = jnp.zeros((1, 1), F32)
    for b in range(FF // TILE):
        s = slice(TILE * b, TILE * (b + 1))
        squares += jnp.sum(jnp.where(on_diagonal, total[s, s], 0.0), keepdims=True)
    inverse = 1.0 / (jnp.sqrt(squares) + norm_epsilon)

    def mirror(b, upper):
        n = TILE * (b + 1)
        gram[0:n, TILE * b : n] = upper
        for a in range(b):
            gram[TILE * b : n, TILE * a : TILE * (a + 1)] = upper[TILE * a : TILE * (a + 1)].T

    for b in range(FF // TILE):
        n = TILE * (b + 1)
        mirror(b, (total[0:n, TILE * b : n] * inverse * inverse).astype(BF16))

    def polynomial():
        g = gram[...]
        square = jnp.dot(g, g, preferred_element_type=F32)
        poly[...] = (cubic_coef * g.astype(F32) + quintic_coef * square).astype(BF16)

    span = DEVICES // BLOCKS

    def apply(current):
        return (
            linear_coef * current.astype(F32)
            + jnp.dot(current, poly[...], preferred_element_type=F32)
        ).astype(BF16)

    polynomial()

    def first(j, carry):
        part = pl.ds(j * span, span)
        start = (rows[part].reshape(span * ROWS, FF).astype(F32) * inverse).astype(BF16)
        rows[part] = apply(start).reshape(span, ROWS, FF)
        return carry

    lax.fori_loop(0, BLOCKS, first, 0)

    whole = rows[...].reshape(DEVICES * ROWS, FF)
    for b in range(FF // TILE):
        n = TILE * (b + 1)
        mirror(
            b,
            lax.dot_general(
                whole[:, 0:n], whole[:, TILE * b : n], TRANSPOSED, preferred_element_type=F32
            ).astype(BF16),
        )
    polynomial()

    full_rows = DEVICES * ROWS

    def send_back(step, c):
        ty, to = chip_at(step, 2 * c - 1)
        pltpu.make_async_remote_copy(
            src_ref=sent.at[2 * step + c],
            dst_ref=update_hbm.at[me],
            send_sem=back_send,
            recv_sem=back_recv,
            device_id=(ty, to + c),
            device_id_type=MESH,
        ).start()

    def last(j, energy):
        part = pl.ds(j * span, span)
        ortho = apply(rows[part].reshape(span * ROWS, FF)).astype(F32)
        sent[part] = (math.sqrt(full_rows) * ortho).astype(BF16).reshape(span, ROWS, FF)
        energy += jnp.sum((ortho * ortho).reshape(-1, 8, FF), axis=0)

        @pl.when(j == 0)
        def _():
            for c in range(CORES):

                @pl.when(core == c)
                def _():
                    pltpu.make_async_copy(sent.at[c], update_hbm.at[me], own_sem.at[1]).start()

                @pl.when(core != c)
                def _():
                    send_back(0, c)

        def one(step, carry):
            for c in range(CORES):
                send_back(step, c)
            return carry

        steps = CHIPS // BLOCKS
        lax.fori_loop(jnp.maximum(j * steps, 1), (j + 1) * steps, one, 0)
        return energy

    energy = lax.fori_loop(0, BLOCKS, last, jnp.zeros((8, FF), F32))
    mean = jnp.sum(energy, keepdims=True) / (full_rows * FF)
    rms = math.sqrt(full_rows) * jnp.sqrt(mean)
    lane = lax.broadcasted_iota(jnp.int32, (1, DEVICES), 1)
    rms_mine[...] = jnp.where(lane == me, rms, 0.0)

    def tell(i, carry):
        t = lax.rem(me + i, DEVICES)
        pltpu.make_async_remote_copy(
            src_ref=rms_mine,
            dst_ref=rms_rows.at[me],
            send_sem=rms_send,
            recv_sem=rms_recv,
            device_id=(lax.div(t, 32), lax.rem(t, 32)),
            device_id_type=MESH,
        ).start()
        return carry

    lax.fori_loop(1, DEVICES, tell, 0)
    pltpu.make_async_copy(rms_mine, rms_rows.at[me], own_sem.at[2]).start()

    others = pl.ds(0, DEVICES - 1)
    pltpu.make_async_copy(rms_mine, rms_rows.at[me], own_sem.at[2]).wait()
    pltpu.make_async_copy(rms_rows.at[others], rms_rows.at[others], rms_recv).wait()
    pltpu.make_async_copy(rms_rows.at[others], rms_rows.at[others], rms_send).wait()

    every = jnp.sum(rms_rows[...], axis=0)
    owned = table_ref[...] == me
    low = jnp.min(jnp.where(owned, lane, DEVICES), keepdims=True)
    high = jnp.max(jnp.where(owned, lane, -1), keepdims=True)
    first_rms = jnp.sum(jnp.where(lane == low, every, 0.0), keepdims=True)
    second_rms = jnp.sum(jnp.where((lane == high) & (high > low), every, 0.0), keepdims=True)
    log_ref[...] = jnp.where(lane == 0, first_rms, jnp.where(lane == 1, second_rms, 0.0))

    for phase in range(CORES):
        for k in range(CHUNKS):
            part = pl.ds(k * per, per)
            pltpu.make_async_copy(
                mv.at[part, phase], fresh_hbm.at[part, phase], fresh_sem.at[phase, k]
            ).wait()
    pltpu.make_async_copy(rows.at[others], rows.at[others], send_sem).wait()
    pltpu.make_async_copy(sent.at[others], sent.at[others], back_send).wait()
    pltpu.make_async_copy(sent.at[0], update_hbm.at[me], own_sem.at[1]).wait()
    pltpu.make_async_copy(update_hbm.at[others], update_hbm.at[others], back_recv).wait()


def on_device(gradient, momentum, owner_table):
    paired = (CHIPS, CORES, ROWS, FF)
    anywhere = pl.BlockSpec(memory_space=pl.ANY)
    in_vmem = pl.BlockSpec(memory_space=pltpu.VMEM)
    fresh, update, log = pl.pallas_call(
        kernel,
        out_shape=(
            jax.ShapeDtypeStruct(paired, F32),
            jax.ShapeDtypeStruct((DEVICES, ROWS, FF), BF16),
            jax.ShapeDtypeStruct((1, DEVICES), F32),
        ),
        in_specs=[anywhere, anywhere, in_vmem],
        out_specs=(anywhere, anywhere, in_vmem),
        scratch_shapes=[
            pltpu.VMEM(paired, BF16),
            pltpu.VMEM(paired, F32),
            pltpu.VMEM((DEVICES, ROWS, FF), BF16),
            pltpu.VMEM((DEVICES, ROWS, FF), BF16),
            pltpu.VMEM((FF, FF), BF16),
            pltpu.VMEM((FF, FF), BF16),
            pltpu.VMEM((FF, FF), F32),
            pltpu.VMEM((DEVICES, 1, DEVICES), F32),
            pltpu.VMEM((1, DEVICES), F32),
            pltpu.SemaphoreType.DMA((2, CORES, CHUNKS)),
            pltpu.SemaphoreType.DMA((CORES, CHUNKS)),
            pltpu.SemaphoreType.DMA,
            pltpu.SemaphoreType.DMA((GROUPS,)),
            pltpu.SemaphoreType.DMA((3,)),
            pltpu.SemaphoreType.DMA,
            pltpu.SemaphoreType.DMA,
            pltpu.SemaphoreType.DMA,
            pltpu.SemaphoreType.DMA,
        ],
        compiler_params=pltpu.CompilerParams(
            collective_id=0, has_side_effects=True, vmem_limit_bytes=40 * 2**20
        ),
        cost_estimate=pl.CostEstimate(
            flops=11 * 10**9, bytes_accessed=18 * 2**20, transcendentals=0
        ),
        name="orthogonalize",
    )(
        gradient.reshape(paired),
        momentum.reshape(paired),
        owner_table.reshape(1, DEVICES),
    )
    return fresh.reshape(momentum.shape), update, log[:, :2]


def solution(mesh):
    split = P(None, AXES, None)
    return jax.shard_map(
        on_device,
        mesh=mesh,
        in_specs=(split, split, P()),
        out_specs=(split, split, P(AXES, None)),
        check_vma=False,
    )
```

```python
import math

import jax
import jax.numpy as jnp
from jax import lax
from jax.experimental import pallas as pl
from jax.experimental.pallas import tpu as pltpu
from jax.sharding import PartitionSpec as P

AXES = ("dp", "owner")
MESH = pl.DeviceIdType.MESH
F32, BF16 = jnp.float32, jnp.bfloat16
TRANSPOSED = (((0,), (0,)), ((), ()))

momentum_decay = 0.95
linear_coef = 3.4445
cubic_coef = -4.775
quintic_coef = 2.0315
norm_epsilon = 1e-07

DEVICES, CHIPS, CORES = 128, 64, 2
ROWS, FF = 16, 768
TILE = 256
CHUNKS = 4
GROUPS = 8
STORES = 4
CAP = 2
HALVES = 2
BLOCKS = CORES * HALVES


def displacement(step):
    n = lax.rem(step * 21, CHIPS)
    return lax.div(n, 16), lax.rem(lax.div(n, 4), 4), lax.rem(n, 4)


def kernel(
    g_hbm, m_hbm, table_hbm, fresh_hbm, update_hbm, log_ref,
    gv, mv, rows, sent, gram, poly, total, rms_rows, rms_mine, table,
    load_sem, fresh_sem, send_sem, recv_sem, own_sem, back_send, back_recv, rms_send, rms_recv,
):
    y, o = lax.axis_index("dp"), lax.axis_index("owner")
    x, z, core = lax.div(o, 8), lax.rem(lax.div(o, 2), 4), lax.rem(o, 2)
    me = y * 32 + o
    sign = 1 - 2 * core

    def chip_at(step, direction):
        dy, dx, dz = displacement(step)
        ty = lax.rem(y + direction * dy + 4, 4)
        tx = lax.rem(x + direction * dx + 4, 4)
        tz = lax.rem(z + direction * dz + 4, 4)
        return ty, tx * 8 + tz * 2

    per = CHIPS // CHUNKS
    loads = []
    for phase in range(CORES):
        for k in range(CHUNKS):
            part = pl.ds(k * per, per)
            pair = (
                pltpu.make_async_copy(
                    g_hbm.at[part, phase], gv.at[part, phase], load_sem.at[0, phase, k]
                ),
                pltpu.make_async_copy(
                    m_hbm.at[part, phase], mv.at[part, phase], load_sem.at[1, phase, k]
                ),
            )
            for copy in pair:
                copy.start()
            loads.append(pair)

    table_copy = pltpu.make_async_copy(table_hbm, table, own_sem.at[3])
    table_copy.start()

    barrier = pltpu.get_barrier_semaphore()

    def greet(i, carry):
        t = lax.rem(me + i, DEVICES)
        pl.semaphore_signal(
            barrier, inc=1, device_id=(lax.div(t, 32), lax.rem(t, 32)), device_id_type=MESH
        )
        return carry

    lax.fori_loop(1, DEVICES, greet, 0)

    def effective(phase):
        for k in range(CHUNKS):
            for copy in loads[phase * CHUNKS + k]:
                copy.wait()

            def one(i, carry):
                grad = gv[i, phase].astype(F32)
                fresh = momentum_decay * mv[i, phase] + grad
                mv[i, phase] = fresh
                gv[i, phase] = (grad + momentum_decay * fresh).astype(BF16)
                return carry

            lax.fori_loop(k * per, (k + 1) * per, one, 0)
            part = pl.ds(k * per, per)
            pltpu.make_async_copy(
                mv.at[part, phase], fresh_hbm.at[part, phase], fresh_sem.at[phase, k]
            ).start()

    def forward(phase):
        mine = y * 16 + x * 4 + z

        @pl.when(core != phase)
        def _():
            pltpu.make_async_remote_copy(
                src_ref=gv.at[mine, phase],
                dst_ref=rows.at[core, 0],
                send_sem=send_sem,
                recv_sem=recv_sem.at[0],
                device_id=(y, x * 8 + z * 2 + phase),
                device_id_type=MESH,
            ).start()

        @pl.when(core == phase)
        def _():
            pltpu.make_async_copy(gv.at[mine, phase], rows.at[core, 0], own_sem.at[0]).start()

        def one(step, carry):
            ty, to = chip_at(step, sign)
            pltpu.make_async_remote_copy(
                src_ref=gv.at[ty * 16 + lax.div(to, 2), phase],
                dst_ref=rows.at[core, step],
                send_sem=send_sem,
                recv_sem=recv_sem.at[lax.div(step, CHIPS // GROUPS)],
                device_id=(ty, to + phase),
                device_id_type=MESH,
            ).start()
            return carry

        lax.fori_loop(1, CHIPS, one, 0)

    effective(0)
    pl.semaphore_wait(barrier, DEVICES - 1)
    forward(0)
    effective(1)
    forward(1)

    size = CHIPS // GROUPS
    total[...] = jnp.zeros_like(total)

    def accumulate(j):
        block = rows[:, pl.ds(j * size, size)].reshape(CORES * size * ROWS, FF)
        flipped = block.T
        for b in range(FF // TILE):
            n = TILE * (b + 1)
            total[0:n, TILE * b : n] += jnp.dot(
                flipped[0:n], block[:, TILE * b : n], preferred_element_type=F32
            )

    pltpu.make_async_copy(rows.at[0, 0], rows.at[0, 0], own_sem.at[0]).wait()
    remote = rows.at[0, pl.ds(0, CORES * size - 1)]
    pltpu.make_async_copy(remote, remote, recv_sem.at[0]).wait()
    accumulate(0)

    def arrive(j, carry):
        part = rows.at[:, pl.ds(j * size, size)]
        pltpu.make_async_copy(part, part, recv_sem.at[j]).wait()
        accumulate(j)
        return carry

    lax.fori_loop(1, GROUPS, arrive, 0)

    on_diagonal = lax.broadcasted_iota(jnp.int32, (TILE, TILE), 0) == lax.broadcasted_iota(
        jnp.int32, (TILE, TILE), 1
    )
    squares = jnp.zeros((1, 1), F32)
    for b in range(FF // TILE):
        s = slice(TILE * b, TILE * (b + 1))
        squares += jnp.sum(jnp.where(on_diagonal, total[s, s], 0.0), keepdims=True)
    inverse = 1.0 / (jnp.sqrt(squares) + norm_epsilon)

    def mirror(b, upper):
        n = TILE * (b + 1)
        gram[0:n, TILE * b : n] = upper
        for a in range(b):
            gram[TILE * b : n, TILE * a : TILE * (a + 1)] = upper[TILE * a : TILE * (a + 1)].T

    for b in range(FF // TILE):
        n = TILE * (b + 1)
        mirror(b, (total[0:n, TILE * b : n] * inverse * inverse).astype(BF16))

    def polynomial():
        g = gram[...]
        square = jnp.dot(g, g, preferred_element_type=F32)
        poly[...] = (cubic_coef * g.astype(F32) + quintic_coef * square).astype(BF16)

    span = CHIPS // HALVES

    def apply(current):
        return (
            linear_coef * current.astype(F32)
            + jnp.dot(current, poly[...], preferred_element_type=F32)
        ).astype(BF16)

    polynomial()

    def first(j, carry):
        core_of, part = lax.div(j, HALVES), pl.ds(lax.rem(j, HALVES) * span, span)
        start = (rows[core_of, part].reshape(span * ROWS, FF).astype(F32) * inverse).astype(BF16)
        rows[core_of, part] = apply(start).reshape(span, ROWS, FF)
        return carry

    lax.fori_loop(0, BLOCKS, first, 0)

    whole = rows[...].reshape(DEVICES * ROWS, FF)
    for b in range(FF // TILE):
        n = TILE * (b + 1)
        mirror(
            b,
            lax.dot_general(
                whole[:, 0:n], whole[:, TILE * b : n], TRANSPOSED, preferred_element_type=F32
            ).astype(BF16),
        )
    polynomial()

    full_rows = DEVICES * ROWS

    def send_back(step, c):
        ty, to = chip_at(step, 2 * c - 1)
        pltpu.make_async_remote_copy(
            src_ref=sent.at[c, step],
            dst_ref=update_hbm.at[me],
            send_sem=back_send,
            recv_sem=back_recv,
            device_id=(ty, to + c),
            device_id_type=MESH,
        ).start()

    def last(j, energy):
        c, half = lax.div(j, HALVES), lax.rem(j, HALVES)
        part = pl.ds(half * span, span)
        ortho = apply(rows[c, part].reshape(span * ROWS, FF)).astype(F32)
        sent[c, part] = (math.sqrt(full_rows) * ortho).astype(BF16).reshape(span, ROWS, FF)
        energy += jnp.sum((ortho * ortho).reshape(-1, 8, FF), axis=0)

        @pl.when((half == 0) & (core == c))
        def _():
            pltpu.make_async_copy(sent.at[c, 0], update_hbm.at[me], own_sem.at[1]).start()

        @pl.when((half == 0) & (core != c))
        def _():
            send_back(0, c)

        def one(step, carry):
            send_back(step, c)
            return carry

        lax.fori_loop(jnp.maximum(half * span, 1), (half + 1) * span, one, 0)
        return energy

    energy = lax.fori_loop(0, BLOCKS, last, jnp.zeros((8, FF), F32))
    mean = jnp.sum(energy, keepdims=True) / (full_rows * FF)
    rms = math.sqrt(full_rows) * jnp.sqrt(mean)
    lane = lax.broadcasted_iota(jnp.int32, (1, DEVICES), 1)
    rms_mine[...] = jnp.where(lane == me, rms, 0.0)

    def tell(i, carry):
        t = lax.rem(me + i, DEVICES)
        pltpu.make_async_remote_copy(
            src_ref=rms_mine,
            dst_ref=rms_rows.at[me],
            send_sem=rms_send,
            recv_sem=rms_recv,
            device_id=(lax.div(t, 32), lax.rem(t, 32)),
            device_id_type=MESH,
        ).start()
        return carry

    lax.fori_loop(1, DEVICES, tell, 0)
    pltpu.make_async_copy(rms_mine, rms_rows.at[me], own_sem.at[2]).start()

    others = pl.ds(0, DEVICES - 1)
    pltpu.make_async_copy(rms_mine, rms_rows.at[me], own_sem.at[2]).wait()
    pltpu.make_async_copy(rms_rows.at[others], rms_rows.at[others], rms_recv).wait()
    pltpu.make_async_copy(rms_rows.at[others], rms_rows.at[others], rms_send).wait()

    every = jnp.sum(rms_rows[...], axis=0)
    table_copy.wait()
    owned = table[...] == me
    low = jnp.min(jnp.where(owned, lane, DEVICES), keepdims=True)
    high = jnp.max(jnp.where(owned, lane, -1), keepdims=True)
    first_rms = jnp.sum(jnp.where(lane == low, every, 0.0), keepdims=True)
    second_rms = jnp.sum(jnp.where((lane == high) & (high > low), every, 0.0), keepdims=True)
    log_ref[...] = jnp.where(lane == 0, first_rms, jnp.where(lane == 1, second_rms, 0.0))

    for phase in range(CORES):
        for k in range(CHUNKS):
            part = pl.ds(k * per, per)
            pltpu.make_async_copy(
                mv.at[part, phase], fresh_hbm.at[part, phase], fresh_sem.at[phase, k]
            ).wait()
    pltpu.make_async_copy(update_hbm.at[others], update_hbm.at[others], send_sem).wait()
    pltpu.make_async_copy(update_hbm.at[others], update_hbm.at[others], back_send).wait()
    pltpu.make_async_copy(sent.at[0, 0], update_hbm.at[me], own_sem.at[1]).wait()
    pltpu.make_async_copy(update_hbm.at[others], update_hbm.at[others], back_recv).wait()


def store(fresh_ref, update_ref, log_ref, fresh_out, update_out, log_out, sem):
    per = DEVICES // STORES
    copies = []
    for k in range(STORES):
        part = pl.ds(k * per, per)
        copies.append(pltpu.make_async_copy(fresh_ref.at[part], fresh_out.at[part], sem.at[0, k]))
        copies.append(pltpu.make_async_copy(update_ref.at[part], update_out.at[part], sem.at[1, k]))
    for copy in copies:
        copy.start()
    log_out[...] = log_ref[:, :CAP]
    for copy in copies:
        copy.wait()


def on_device(gradient, momentum, owner_table):
    paired = (CHIPS, CORES, ROWS, FF)
    anywhere = pl.BlockSpec(memory_space=pl.ANY)
    in_vmem = pl.BlockSpec(memory_space=pltpu.VMEM)
    in_hbm = pl.BlockSpec(memory_space=pltpu.HBM)
    fresh, update, log = pl.pallas_call(
        kernel,
        out_shape=(
            jax.ShapeDtypeStruct(paired, F32),
            jax.ShapeDtypeStruct((DEVICES, ROWS, FF), BF16),
            jax.ShapeDtypeStruct((1, DEVICES), F32),
        ),
        in_specs=[in_hbm, in_hbm, in_hbm],
        out_specs=(anywhere, anywhere, in_vmem),
        scratch_shapes=[
            pltpu.VMEM(paired, BF16),
            pltpu.VMEM(paired, F32),
            pltpu.VMEM((CORES, CHIPS, ROWS, FF), BF16),
            pltpu.VMEM((CORES, CHIPS, ROWS, FF), BF16),
            pltpu.VMEM((FF, FF), BF16),
            pltpu.VMEM((FF, FF), BF16),
            pltpu.VMEM((FF, FF), F32),
            pltpu.VMEM((DEVICES, 1, DEVICES), F32),
            pltpu.VMEM((1, DEVICES), F32),
            pltpu.VMEM((1, DEVICES), jnp.int32),
            pltpu.SemaphoreType.DMA((2, CORES, CHUNKS)),
            pltpu.SemaphoreType.DMA((CORES, CHUNKS)),
            pltpu.SemaphoreType.DMA,
            pltpu.SemaphoreType.DMA((GROUPS,)),
            pltpu.SemaphoreType.DMA((4,)),
            pltpu.SemaphoreType.DMA,
            pltpu.SemaphoreType.DMA,
            pltpu.SemaphoreType.DMA,
            pltpu.SemaphoreType.DMA,
        ],
        compiler_params=pltpu.CompilerParams(
            collective_id=0, has_side_effects=True, vmem_limit_bytes=40 * 2**20
        ),
        cost_estimate=pl.CostEstimate(
            flops=11 * 10**9, bytes_accessed=18 * 2**20, transcendentals=0
        ),
        name="orthogonalize",
    )(
        pltpu.with_memory_space_constraint(gradient.reshape(paired), pltpu.HBM),
        pltpu.with_memory_space_constraint(momentum.reshape(paired), pltpu.HBM),
        pltpu.with_memory_space_constraint(owner_table.reshape(1, DEVICES), pltpu.HBM),
    )
    return pl.pallas_call(
        store,
        out_shape=(
            jax.ShapeDtypeStruct(momentum.shape, F32),
            jax.ShapeDtypeStruct(update.shape, BF16),
            jax.ShapeDtypeStruct((1, CAP), F32),
        ),
        in_specs=[anywhere, anywhere, in_vmem],
        out_specs=(in_hbm, in_hbm, in_vmem),
        scratch_shapes=[pltpu.SemaphoreType.DMA((2, STORES))],
        compiler_params=pltpu.CompilerParams(vmem_limit_bytes=2**20),
        name="store",
    )(fresh.reshape(momentum.shape), update, log)


def solution(mesh):
    split = P(None, AXES, None)
    return jax.shard_map(
        on_device,
        mesh=mesh,
        in_specs=(split, split, P()),
        out_specs=(split, split, P(AXES, None)),
        check_vma=False,
    )
```

```python
import math

import jax
import jax.numpy as jnp
from jax import lax
from jax.experimental import pallas as pl
from jax.experimental.pallas import tpu as pltpu
from jax.sharding import PartitionSpec as P

AXES = ("dp", "owner")
MESH = pl.DeviceIdType.MESH
F32, BF16 = jnp.float32, jnp.bfloat16
TRANSPOSED = (((0,), (0,)), ((), ()))

momentum_decay = 0.95
linear_coef = 3.4445
cubic_coef = -4.775
quintic_coef = 2.0315
norm_epsilon = 1e-07

DEVICES, CHIPS, CORES = 128, 64, 2
ROWS, FF = 16, 768
TILE = 256
CHUNKS = 4
GROUPS = 8
STORES = 4
CAP = 2
HALVES = 2
BLOCKS = CORES * HALVES


def displacement(step):
    n = lax.rem(step * 21, CHIPS)
    return lax.div(n, 16), lax.rem(lax.div(n, 4), 4), lax.rem(n, 4)


def kernel(
    g_hbm, m_hbm, table_hbm, fresh_hbm, update_hbm, log_ref,
    gv, mv, rows, sent, gram, poly, total, rms_rows, table,
    load_sem, fresh_sem, send_sem, recv_sem, own_sem, back_send, back_recv, rms_send, rms_recv,
):
    y, o = lax.axis_index("dp"), lax.axis_index("owner")
    x, z, core = lax.div(o, 8), lax.rem(lax.div(o, 2), 4), lax.rem(o, 2)
    me = y * 32 + o
    sign = 1 - 2 * core

    def chip_at(step, direction):
        dy, dx, dz = displacement(step)
        ty = lax.rem(y + direction * dy + 4, 4)
        tx = lax.rem(x + direction * dx + 4, 4)
        tz = lax.rem(z + direction * dz + 4, 4)
        return ty, tx * 8 + tz * 2

    per = CHIPS // CHUNKS
    loads = []
    for phase in range(CORES):
        for k in range(CHUNKS):
            part = pl.ds(k * per, per)
            pair = (
                pltpu.make_async_copy(
                    g_hbm.at[part, phase], gv.at[part, phase], load_sem.at[0, phase, k]
                ),
                pltpu.make_async_copy(
                    m_hbm.at[part, phase], mv.at[part, phase], load_sem.at[1, phase, k]
                ),
            )
            for copy in pair:
                copy.start()
            loads.append(pair)

    table_copy = pltpu.make_async_copy(table_hbm, table, own_sem.at[2])
    table_copy.start()

    barrier = pltpu.get_barrier_semaphore()

    def greet(i, carry):
        t = lax.rem(me + i, DEVICES)
        pl.semaphore_signal(
            barrier, inc=1, device_id=(lax.div(t, 32), lax.rem(t, 32)), device_id_type=MESH
        )
        return carry

    lax.fori_loop(1, DEVICES, greet, 0)

    def effective(phase):
        for k in range(CHUNKS):
            for copy in loads[phase * CHUNKS + k]:
                copy.wait()

            def one(i, carry):
                grad = gv[i, phase].astype(F32)
                fresh = momentum_decay * mv[i, phase] + grad
                mv[i, phase] = fresh
                gv[i, phase] = (grad + momentum_decay * fresh).astype(BF16)
                return carry

            lax.fori_loop(k * per, (k + 1) * per, one, 0)
            part = pl.ds(k * per, per)
            pltpu.make_async_copy(
                mv.at[part, phase], fresh_hbm.at[part, phase], fresh_sem.at[phase, k]
            ).start()

    def forward(phase):
        mine = y * 16 + x * 4 + z

        @pl.when(core != phase)
        def _():
            pltpu.make_async_remote_copy(
                src_ref=gv.at[mine, phase],
                dst_ref=rows.at[core, 0],
                send_sem=send_sem,
                recv_sem=recv_sem.at[0],
                device_id=(y, x * 8 + z * 2 + phase),
                device_id_type=MESH,
            ).start()

        @pl.when(core == phase)
        def _():
            pltpu.make_async_copy(gv.at[mine, phase], rows.at[core, 0], own_sem.at[0]).start()

        def one(step, carry):
            ty, to = chip_at(step, sign)
            pltpu.make_async_remote_copy(
                src_ref=gv.at[ty * 16 + lax.div(to, 2), phase],
                dst_ref=rows.at[core, step],
                send_sem=send_sem,
                recv_sem=recv_sem.at[lax.div(step, CHIPS // GROUPS)],
                device_id=(ty, to + phase),
                device_id_type=MESH,
            ).start()
            return carry

        lax.fori_loop(1, CHIPS, one, 0)

    effective(0)
    pl.semaphore_wait(barrier, DEVICES - 1)
    forward(0)
    effective(1)
    forward(1)

    size = CHIPS // GROUPS
    total[...] = jnp.zeros_like(total)

    def accumulate(j):
        block = rows[:, pl.ds(j * size, size)].reshape(CORES * size * ROWS, FF)
        flipped = block.T
        for b in range(FF // TILE):
            n = TILE * (b + 1)
            total[0:n, TILE * b : n] += jnp.dot(
                flipped[0:n], block[:, TILE * b : n], preferred_element_type=F32
            )

    pltpu.make_async_copy(rows.at[0, 0], rows.at[0, 0], own_sem.at[0]).wait()
    remote = rows.at[0, pl.ds(0, CORES * size - 1)]
    pltpu.make_async_copy(remote, remote, recv_sem.at[0]).wait()
    accumulate(0)

    def arrive(j, carry):
        part = rows.at[:, pl.ds(j * size, size)]
        pltpu.make_async_copy(part, part, recv_sem.at[j]).wait()
        accumulate(j)
        return carry

    lax.fori_loop(1, GROUPS, arrive, 0)

    on_diagonal = lax.broadcasted_iota(jnp.int32, (TILE, TILE), 0) == lax.broadcasted_iota(
        jnp.int32, (TILE, TILE), 1
    )
    squares = jnp.zeros((1, 1), F32)
    for b in range(FF // TILE):
        s = slice(TILE * b, TILE * (b + 1))
        squares += jnp.sum(jnp.where(on_diagonal, total[s, s], 0.0), keepdims=True)
    inverse = 1.0 / (jnp.sqrt(squares) + norm_epsilon)

    def mirror(b, upper):
        n = TILE * (b + 1)
        gram[0:n, TILE * b : n] = upper
        for a in range(b):
            gram[TILE * b : n, TILE * a : TILE * (a + 1)] = upper[TILE * a : TILE * (a + 1)].T

    for b in range(FF // TILE):
        n = TILE * (b + 1)
        mirror(b, (total[0:n, TILE * b : n] * inverse * inverse).astype(BF16))

    def polynomial():
        g = gram[...]
        square = jnp.dot(g, g, preferred_element_type=F32)
        poly[...] = (cubic_coef * g.astype(F32) + quintic_coef * square).astype(BF16)

    span = CHIPS // HALVES

    def apply(current):
        return (
            linear_coef * current.astype(F32)
            + jnp.dot(current, poly[...], preferred_element_type=F32)
        ).astype(BF16)

    polynomial()

    def first(j, carry):
        core_of, part = lax.div(j, HALVES), pl.ds(lax.rem(j, HALVES) * span, span)
        start = (rows[core_of, part].reshape(span * ROWS, FF).astype(F32) * inverse).astype(BF16)
        rows[core_of, part] = apply(start).reshape(span, ROWS, FF)
        return carry

    lax.fori_loop(0, BLOCKS, first, 0)

    whole = rows[...].reshape(DEVICES * ROWS, FF)
    for b in range(FF // TILE):
        n = TILE * (b + 1)
        mirror(
            b,
            lax.dot_general(
                whole[:, 0:n], whole[:, TILE * b : n], TRANSPOSED, preferred_element_type=F32
            ).astype(BF16),
        )
    polynomial()

    full_rows = DEVICES * ROWS

    lane = lax.broadcasted_iota(jnp.int32, (1, DEVICES), 1)

    def send_back(step, c):
        ty, to = chip_at(step, 2 * c - 1)
        pltpu.make_async_remote_copy(
            src_ref=sent.at[c, step],
            dst_ref=update_hbm.at[me],
            send_sem=back_send,
            recv_sem=back_recv,
            device_id=(ty, to + c),
            device_id_type=MESH,
        ).start()

    def send_half(c, half):
        if half == 0:

            @pl.when(core == c)
            def _():
                pltpu.make_async_copy(sent.at[c, 0], update_hbm.at[me], own_sem.at[1]).start()

            @pl.when(core != c)
            def _():
                send_back(0, c)

        def one(step, carry):
            send_back(step, c)
            return carry

        lax.fori_loop(max(half * span, 1), (half + 1) * span, one, 0)

    def last(j, energy):
        c, half = lax.div(j, HALVES), lax.rem(j, HALVES)
        part = pl.ds(half * span, span)
        ortho = apply(rows[c, part].reshape(span * ROWS, FF)).astype(F32)
        sent[c, part] = (math.sqrt(full_rows) * ortho).astype(BF16).reshape(span, ROWS, FF)
        energy += jnp.sum((ortho * ortho).reshape(-1, 8, FF), axis=0)
        pl.when(j == 0)(lambda: send_half(0, 0))
        return energy

    energy = lax.fori_loop(0, BLOCKS, last, jnp.zeros((8, FF), F32))
    mean = jnp.sum(energy, keepdims=True) / (full_rows * FF)
    rms = math.sqrt(full_rows) * jnp.sqrt(mean)
    rms_rows[me] = jnp.where(lane == me, rms, 0.0)

    column, place = lax.div(me, 8), lax.rem(me, 8)
    mine_too = pl.ds(column * 8, 8)
    for i in range(1, 8):
        pltpu.make_async_remote_copy(
            src_ref=rms_rows.at[me],
            dst_ref=rms_rows.at[me],
            send_sem=rms_send.at[0],
            recv_sem=rms_recv.at[0],
            device_id=(y, x * 8 + lax.rem(place + i, 8)),
            device_id_type=MESH,
        ).start()

    def spread():
        seven = rms_rows.at[pl.ds(0, 7)]
        pltpu.make_async_copy(seven, seven, rms_recv.at[0]).wait()
        for i in range(1, 16):
            other = lax.rem(column + i, 16)
            pltpu.make_async_remote_copy(
                src_ref=rms_rows.at[mine_too],
                dst_ref=rms_rows.at[mine_too],
                send_sem=rms_send.at[1],
                recv_sem=rms_recv.at[1],
                device_id=(lax.div(other, 4), lax.rem(other, 4) * 8 + place),
                device_id_type=MESH,
            ).start()

    send_half(0, 1)

    @pl.when(core == 0)
    def _():
        send_half(1, 0)
        send_half(1, 1)
        spread()

    @pl.when(core == 1)
    def _():
        spread()
        send_half(1, 0)
        send_half(1, 1)

    others = pl.ds(0, DEVICES - 1)
    for stage, count in ((0, 7), (1, DEVICES - 8)):
        part = rms_rows.at[pl.ds(0, count)]
        pltpu.make_async_copy(part, part, rms_send.at[stage]).wait()
        if stage:
            pltpu.make_async_copy(part, part, rms_recv.at[stage]).wait()

    every = jnp.sum(rms_rows[...], axis=0)
    table_copy.wait()
    owned = table[...] == me
    low = jnp.min(jnp.where(owned, lane, DEVICES), keepdims=True)
    high = jnp.max(jnp.where(owned, lane, -1), keepdims=True)
    first_rms = jnp.sum(jnp.where(lane == low, every, 0.0), keepdims=True)
    second_rms = jnp.sum(jnp.where((lane == high) & (high > low), every, 0.0), keepdims=True)
    log_ref[...] = jnp.where(lane == 0, first_rms, jnp.where(lane == 1, second_rms, 0.0))

    for phase in range(CORES):
        for k in range(CHUNKS):
            part = pl.ds(k * per, per)
            pltpu.make_async_copy(
                mv.at[part, phase], fresh_hbm.at[part, phase], fresh_sem.at[phase, k]
            ).wait()
    pltpu.make_async_copy(update_hbm.at[others], update_hbm.at[others], send_sem).wait()
    pltpu.make_async_copy(update_hbm.at[others], update_hbm.at[others], back_send).wait()
    pltpu.make_async_copy(sent.at[0, 0], update_hbm.at[me], own_sem.at[1]).wait()
    pltpu.make_async_copy(update_hbm.at[others], update_hbm.at[others], back_recv).wait()


def store(fresh_ref, update_ref, log_ref, fresh_out, update_out, log_out, sem):
    per = DEVICES // STORES
    copies = []
    for k in range(STORES):
        part = pl.ds(k * per, per)
        copies.append(pltpu.make_async_copy(fresh_ref.at[part], fresh_out.at[part], sem.at[0, k]))
        copies.append(pltpu.make_async_copy(update_ref.at[part], update_out.at[part], sem.at[1, k]))
    for copy in copies:
        copy.start()
    log_out[...] = log_ref[:, :CAP]
    for copy in copies:
        copy.wait()


def on_device(gradient, momentum, owner_table):
    paired = (CHIPS, CORES, ROWS, FF)
    anywhere = pl.BlockSpec(memory_space=pl.ANY)
    in_vmem = pl.BlockSpec(memory_space=pltpu.VMEM)
    in_hbm = pl.BlockSpec(memory_space=pltpu.HBM)
    fresh, update, log = pl.pallas_call(
        kernel,
        out_shape=(
            jax.ShapeDtypeStruct(paired, F32),
            jax.ShapeDtypeStruct((DEVICES, ROWS, FF), BF16),
            jax.ShapeDtypeStruct((1, DEVICES), F32),
        ),
        in_specs=[in_hbm, in_hbm, in_hbm],
        out_specs=(anywhere, anywhere, in_vmem),
        scratch_shapes=[
            pltpu.VMEM(paired, BF16),
            pltpu.VMEM(paired, F32),
            pltpu.VMEM((CORES, CHIPS, ROWS, FF), BF16),
            pltpu.VMEM((CORES, CHIPS, ROWS, FF), BF16),
            pltpu.VMEM((FF, FF), BF16),
            pltpu.VMEM((FF, FF), BF16),
            pltpu.VMEM((FF, FF), F32),
            pltpu.VMEM((DEVICES, 1, DEVICES), F32),
            pltpu.VMEM((1, DEVICES), jnp.int32),
            pltpu.SemaphoreType.DMA((2, CORES, CHUNKS)),
            pltpu.SemaphoreType.DMA((CORES, CHUNKS)),
            pltpu.SemaphoreType.DMA,
            pltpu.SemaphoreType.DMA((GROUPS,)),
            pltpu.SemaphoreType.DMA((3,)),
            pltpu.SemaphoreType.DMA,
            pltpu.SemaphoreType.DMA,
            pltpu.SemaphoreType.DMA((2,)),
            pltpu.SemaphoreType.DMA((2,)),
        ],
        compiler_params=pltpu.CompilerParams(
            collective_id=0, has_side_effects=True, vmem_limit_bytes=40 * 2**20
        ),
        cost_estimate=pl.CostEstimate(
            flops=11 * 10**9, bytes_accessed=18 * 2**20, transcendentals=0
        ),
        name="orthogonalize",
    )(
        pltpu.with_memory_space_constraint(gradient.reshape(paired), pltpu.HBM),
        pltpu.with_memory_space_constraint(momentum.reshape(paired), pltpu.HBM),
        pltpu.with_memory_space_constraint(owner_table.reshape(1, DEVICES), pltpu.HBM),
    )
    return pl.pallas_call(
        store,
        out_shape=(
            jax.ShapeDtypeStruct(momentum.shape, F32),
            jax.ShapeDtypeStruct(update.shape, BF16),
            jax.ShapeDtypeStruct((1, CAP), F32),
        ),
        in_specs=[anywhere, anywhere, in_vmem],
        out_specs=(in_hbm, in_hbm, in_vmem),
        scratch_shapes=[pltpu.SemaphoreType.DMA((2, STORES))],
        compiler_params=pltpu.CompilerParams(vmem_limit_bytes=2**20),
        name="store",
    )(fresh.reshape(momentum.shape), update, log)


def solution(mesh):
    split = P(None, AXES, None)
    return jax.shard_map(
        on_device,
        mesh=mesh,
        in_specs=(split, split, P()),
        out_specs=(split, split, P(AXES, None)),
        check_vma=False,
    )
```

```python
import math

import jax
import jax.numpy as jnp
from jax import lax
from jax.experimental import pallas as pl
from jax.experimental.pallas import tpu as pltpu
from jax.sharding import PartitionSpec as P

AXES = ("dp", "owner")
MESH = pl.DeviceIdType.MESH
F32, BF16 = jnp.float32, jnp.bfloat16
TRANSPOSED = (((0,), (0,)), ((), ()))

momentum_decay = 0.95
linear_coef = 3.4445
cubic_coef = -4.775
quintic_coef = 2.0315
norm_epsilon = 1e-07

DEVICES, CHIPS, CORES = 128, 64, 2
ROWS, FF = 16, 768
TILE = 256
CHUNKS = 4
GROUPS = 8
STORES = 4
CAP = 2
HALVES = 2
BLOCKS = CORES * HALVES


def displacement(step):
    n = lax.rem(step * 21, CHIPS)
    return lax.div(n, 16), lax.rem(lax.div(n, 4), 4), lax.rem(n, 4)


def kernel(
    g_hbm, m_hbm, table_hbm, fresh_hbm, update_hbm, log_hbm,
    gv, mv, rows, sent, gram, poly, total, rms_rows, table, log,
    load_sem, fresh_sem, send_sem, recv_sem, own_sem, back_send, back_recv, rms_send, rms_recv,
):
    y, o = lax.axis_index("dp"), lax.axis_index("owner")
    x, z, core = lax.div(o, 8), lax.rem(lax.div(o, 2), 4), lax.rem(o, 2)
    me = y * 32 + o
    sign = 1 - 2 * core

    def chip_at(step, direction):
        dy, dx, dz = displacement(step)
        ty = lax.rem(y + direction * dy + 4, 4)
        tx = lax.rem(x + direction * dx + 4, 4)
        tz = lax.rem(z + direction * dz + 4, 4)
        return ty, tx * 8 + tz * 2

    barrier = pltpu.get_barrier_semaphore()

    def greet(i, carry):
        t = lax.rem(me + i, DEVICES)
        pl.semaphore_signal(
            barrier, inc=1, device_id=(lax.div(t, 32), lax.rem(t, 32)), device_id_type=MESH
        )
        return carry

    lax.fori_loop(1, DEVICES, greet, 0)

    per = CHIPS // CHUNKS
    loads = []
    for phase in range(CORES):
        for k in range(CHUNKS):
            part = pl.ds(k * per, per)
            pair = (
                pltpu.make_async_copy(
                    g_hbm.at[part, phase], gv.at[part, phase], load_sem.at[0, phase, k]
                ),
                pltpu.make_async_copy(
                    m_hbm.at[part, phase], mv.at[part, phase], load_sem.at[1, phase, k]
                ),
            )
            for copy in pair:
                copy.start()
            loads.append(pair)

    table_copy = pltpu.make_async_copy(table_hbm, table, own_sem.at[2])
    table_copy.start()

    def effective(phase):
        for k in range(CHUNKS):
            for copy in loads[phase * CHUNKS + k]:
                copy.wait()

            def one(i, carry):
                grad = gv[i, phase].astype(F32)
                fresh = momentum_decay * mv[i, phase] + grad
                mv[i, phase] = fresh
                gv[i, phase] = (grad + momentum_decay * fresh).astype(BF16)
                return carry

            lax.fori_loop(k * per, (k + 1) * per, one, 0)
            part = pl.ds(k * per, per)
            pltpu.make_async_copy(
                mv.at[part, phase], fresh_hbm.at[part, phase], fresh_sem.at[phase, k]
            ).start()

    def forward(phase):
        mine = y * 16 + x * 4 + z

        @pl.when(core != phase)
        def _():
            pltpu.make_async_remote_copy(
                src_ref=gv.at[mine, phase],
                dst_ref=rows.at[core, 0],
                send_sem=send_sem,
                recv_sem=recv_sem.at[0],
                device_id=(y, x * 8 + z * 2 + phase),
                device_id_type=MESH,
            ).start()

        @pl.when(core == phase)
        def _():
            pltpu.make_async_copy(gv.at[mine, phase], rows.at[core, 0], own_sem.at[0]).start()

        def one(step, carry):
            ty, to = chip_at(step, sign)
            pltpu.make_async_remote_copy(
                src_ref=gv.at[ty * 16 + lax.div(to, 2), phase],
                dst_ref=rows.at[core, step],
                send_sem=send_sem,
                recv_sem=recv_sem.at[lax.div(step, CHIPS // GROUPS)],
                device_id=(ty, to + phase),
                device_id_type=MESH,
            ).start()
            return carry

        lax.fori_loop(1, CHIPS, one, 0)

    effective(0)
    pl.semaphore_wait(barrier, DEVICES - 1)
    forward(0)
    effective(1)
    forward(1)

    size = CHIPS // GROUPS
    total[...] = jnp.zeros_like(total)

    def accumulate(j):
        block = rows[:, pl.ds(j * size, size)].reshape(CORES * size * ROWS, FF)
        flipped = block.T
        for b in range(FF // TILE):
            n = TILE * (b + 1)
            total[0:n, TILE * b : n] += jnp.dot(
                flipped[0:n], block[:, TILE * b : n], preferred_element_type=F32
            )

    pltpu.make_async_copy(rows.at[0, 0], rows.at[0, 0], own_sem.at[0]).wait()
    remote = rows.at[0, pl.ds(0, CORES * size - 1)]
    pltpu.make_async_copy(remote, remote, recv_sem.at[0]).wait()
    accumulate(0)

    def arrive(j, carry):
        part = rows.at[:, pl.ds(j * size, size)]
        pltpu.make_async_copy(part, part, recv_sem.at[j]).wait()
        accumulate(j)
        return carry

    lax.fori_loop(1, GROUPS, arrive, 0)

    on_diagonal = lax.broadcasted_iota(jnp.int32, (TILE, TILE), 0) == lax.broadcasted_iota(
        jnp.int32, (TILE, TILE), 1
    )
    squares = jnp.zeros((1, 1), F32)
    for b in range(FF // TILE):
        s = slice(TILE * b, TILE * (b + 1))
        squares += jnp.sum(jnp.where(on_diagonal, total[s, s], 0.0), keepdims=True)
    inverse = 1.0 / (jnp.sqrt(squares) + norm_epsilon)

    def mirror(ref, b, upper):
        n = TILE * (b + 1)
        ref[0:n, TILE * b : n] = upper
        for a in range(b):
            ref[TILE * b : n, TILE * a : TILE * (a + 1)] = upper[TILE * a : TILE * (a + 1)].T

    for b in range(FF // TILE):
        n = TILE * (b + 1)
        mirror(gram, b, (total[0:n, TILE * b : n] * inverse * inverse).astype(BF16))

    def polynomial():
        for b in range(FF // TILE):
            n = TILE * (b + 1)
            square = jnp.dot(gram[0:n, :], gram[:, TILE * b : n], preferred_element_type=F32)
            upper = (
                cubic_coef * gram[0:n, TILE * b : n].astype(F32) + quintic_coef * square
            ).astype(BF16)
            mirror(poly, b, upper)

    span = CHIPS // HALVES

    def apply(current):
        return (
            linear_coef * current.astype(F32)
            + jnp.dot(current, poly[...], preferred_element_type=F32)
        ).astype(BF16)

    polynomial()

    def first(c, carry):
        start = (rows[c].reshape(CHIPS * ROWS, FF).astype(F32) * inverse).astype(BF16)
        rows[c] = apply(start).reshape(CHIPS, ROWS, FF)
        return carry

    lax.fori_loop(0, CORES, first, 0)

    whole = rows[...].reshape(DEVICES * ROWS, FF)
    for b in range(FF // TILE):
        n = TILE * (b + 1)
        mirror(
            gram,
            b,
            lax.dot_general(
                whole[:, 0:n], whole[:, TILE * b : n], TRANSPOSED, preferred_element_type=F32
            ).astype(BF16),
        )
    polynomial()

    full_rows = DEVICES * ROWS

    lane = lax.broadcasted_iota(jnp.int32, (1, DEVICES), 1)

    def send_back(step, c):
        ty, to = chip_at(step, 2 * c - 1)
        pltpu.make_async_remote_copy(
            src_ref=sent.at[c, step],
            dst_ref=update_hbm.at[me],
            send_sem=back_send,
            recv_sem=back_recv,
            device_id=(ty, to + c),
            device_id_type=MESH,
        ).start()

    def send_half(c, half):
        if half == 0:

            @pl.when(core == c)
            def _():
                pltpu.make_async_copy(sent.at[c, 0], update_hbm.at[me], own_sem.at[1]).start()

            @pl.when(core != c)
            def _():
                send_back(0, c)

        def one(step, carry):
            send_back(step, c)
            return carry

        lax.fori_loop(max(half * span, 1), (half + 1) * span, one, 0)

    def last(j, energy):
        c, half = lax.div(j, HALVES), lax.rem(j, HALVES)
        part = pl.ds(half * span, span)
        ortho = apply(rows[c, part].reshape(span * ROWS, FF)).astype(F32)
        sent[c, part] = (math.sqrt(full_rows) * ortho).astype(BF16).reshape(span, ROWS, FF)
        energy += jnp.sum((ortho * ortho).reshape(-1, 8, FF), axis=0)
        pl.when(j == 0)(lambda: send_half(0, 0))
        return energy

    energy = lax.fori_loop(0, BLOCKS, last, jnp.zeros((8, FF), F32))
    mean = jnp.sum(energy, keepdims=True) / (full_rows * FF)
    rms = math.sqrt(full_rows) * jnp.sqrt(mean)
    rms_rows[me] = jnp.where(lane == me, rms, 0.0)

    column, place = lax.div(me, 8), lax.rem(me, 8)
    mine_too = pl.ds(column * 8, 8)
    for i in range(1, 8):
        pltpu.make_async_remote_copy(
            src_ref=rms_rows.at[me],
            dst_ref=rms_rows.at[me],
            send_sem=rms_send.at[0],
            recv_sem=rms_recv.at[0],
            device_id=(y, x * 8 + lax.rem(place + i, 8)),
            device_id_type=MESH,
        ).start()

    def spread():
        seven = rms_rows.at[pl.ds(0, 7)]
        pltpu.make_async_copy(seven, seven, rms_recv.at[0]).wait()
        for i in range(1, 16):
            other = lax.rem(column + i, 16)
            pltpu.make_async_remote_copy(
                src_ref=rms_rows.at[mine_too],
                dst_ref=rms_rows.at[mine_too],
                send_sem=rms_send.at[1],
                recv_sem=rms_recv.at[1],
                device_id=(lax.div(other, 4), lax.rem(other, 4) * 8 + place),
                device_id_type=MESH,
            ).start()

    send_half(0, 1)

    @pl.when(core == 0)
    def _():
        send_half(1, 0)
        send_half(1, 1)
        spread()

    @pl.when(core == 1)
    def _():
        spread()
        send_half(1, 0)
        send_half(1, 1)

    others = pl.ds(0, DEVICES - 1)
    for stage, count in ((0, 7), (1, DEVICES - 8)):
        part = rms_rows.at[pl.ds(0, count)]
        pltpu.make_async_copy(part, part, rms_send.at[stage]).wait()
        if stage:
            pltpu.make_async_copy(part, part, rms_recv.at[stage]).wait()

    every = jnp.sum(rms_rows[...], axis=0)
    table_copy.wait()
    owned = table[...] == me
    low = jnp.min(jnp.where(owned, lane, DEVICES), keepdims=True)
    high = jnp.max(jnp.where(owned, lane, -1), keepdims=True)
    first_rms = jnp.sum(jnp.where(lane == low, every, 0.0), keepdims=True)
    second_rms = jnp.sum(jnp.where((lane == high) & (high > low), every, 0.0), keepdims=True)
    log[...] = jnp.where(lane == 0, first_rms, jnp.where(lane == 1, second_rms, 0.0))[:, :CAP]
    log_copy = pltpu.make_async_copy(log, log_hbm, own_sem.at[3])
    log_copy.start()

    for phase in range(CORES):
        for k in range(CHUNKS):
            part = pl.ds(k * per, per)
            pltpu.make_async_copy(
                mv.at[part, phase], fresh_hbm.at[part, phase], fresh_sem.at[phase, k]
            ).wait()
    pltpu.make_async_copy(update_hbm.at[others], update_hbm.at[others], send_sem).wait()
    pltpu.make_async_copy(update_hbm.at[others], update_hbm.at[others], back_send).wait()
    pltpu.make_async_copy(sent.at[0, 0], update_hbm.at[me], own_sem.at[1]).wait()
    pltpu.make_async_copy(update_hbm.at[others], update_hbm.at[others], back_recv).wait()
    log_copy.wait()


def store(fresh_ref, update_ref, log_ref, fresh_out, update_out, log_out, sem):
    per = DEVICES // STORES
    copies = [pltpu.make_async_copy(log_ref, log_out, sem.at[2, 0])]
    for k in range(STORES):
        part = pl.ds(k * per, per)
        copies.append(pltpu.make_async_copy(fresh_ref.at[part], fresh_out.at[part], sem.at[0, k]))
        copies.append(pltpu.make_async_copy(update_ref.at[part], update_out.at[part], sem.at[1, k]))
    for copy in copies:
        copy.start()
    for copy in copies:
        copy.wait()


def on_device(gradient, momentum, owner_table):
    paired = (CHIPS, CORES, ROWS, FF)
    anywhere = pl.BlockSpec(memory_space=pl.ANY)
    in_hbm = pl.BlockSpec(memory_space=pltpu.HBM)
    fresh, update, log = pl.pallas_call(
        kernel,
        out_shape=(
            jax.ShapeDtypeStruct(paired, F32),
            jax.ShapeDtypeStruct((DEVICES, ROWS, FF), BF16),
            jax.ShapeDtypeStruct((1, CAP), F32),
        ),
        in_specs=[in_hbm, in_hbm, in_hbm],
        out_specs=(anywhere, anywhere, anywhere),
        scratch_shapes=[
            pltpu.VMEM(paired, BF16),
            pltpu.VMEM(paired, F32),
            pltpu.VMEM((CORES, CHIPS, ROWS, FF), BF16),
            pltpu.VMEM((CORES, CHIPS, ROWS, FF), BF16),
            pltpu.VMEM((FF, FF), BF16),
            pltpu.VMEM((FF, FF), BF16),
            pltpu.VMEM((FF, FF), F32),
            pltpu.VMEM((DEVICES, 1, DEVICES), F32),
            pltpu.VMEM((1, DEVICES), jnp.int32),
            pltpu.VMEM((1, CAP), F32),
            pltpu.SemaphoreType.DMA((2, CORES, CHUNKS)),
            pltpu.SemaphoreType.DMA((CORES, CHUNKS)),
            pltpu.SemaphoreType.DMA,
            pltpu.SemaphoreType.DMA((GROUPS,)),
            pltpu.SemaphoreType.DMA((4,)),
            pltpu.SemaphoreType.DMA,
            pltpu.SemaphoreType.DMA,
            pltpu.SemaphoreType.DMA((2,)),
            pltpu.SemaphoreType.DMA((2,)),
        ],
        compiler_params=pltpu.CompilerParams(
            collective_id=0, has_side_effects=True, vmem_limit_bytes=40 * 2**20
        ),
        cost_estimate=pl.CostEstimate(
            flops=11 * 10**9, bytes_accessed=18 * 2**20, transcendentals=0
        ),
        name="orthogonalize",
    )(
        pltpu.with_memory_space_constraint(gradient.reshape(paired), pltpu.HBM),
        pltpu.with_memory_space_constraint(momentum.reshape(paired), pltpu.HBM),
        pltpu.with_memory_space_constraint(owner_table.reshape(1, DEVICES), pltpu.HBM),
    )
    return pl.pallas_call(
        store,
        out_shape=(
            jax.ShapeDtypeStruct(momentum.shape, F32),
            jax.ShapeDtypeStruct(update.shape, BF16),
            jax.ShapeDtypeStruct((1, CAP), F32),
        ),
        in_specs=[anywhere, anywhere, anywhere],
        out_specs=(in_hbm, in_hbm, in_hbm),
        scratch_shapes=[pltpu.SemaphoreType.DMA((3, STORES))],
        compiler_params=pltpu.CompilerParams(vmem_limit_bytes=2**20),
        name="store",
    )(fresh.reshape(momentum.shape), update, log)


def solution(mesh):
    split = P(None, AXES, None)
    return jax.shard_map(
        on_device,
        mesh=mesh,
        in_specs=(split, split, P()),
        out_specs=(split, split, P(AXES, None)),
        check_vma=False,
    )
```

```python
import math

import jax
import jax.numpy as jnp
from jax import lax
from jax.experimental import pallas as pl
from jax.experimental.pallas import tpu as pltpu
from jax.sharding import PartitionSpec as P

AXES = ("dp", "owner")
MESH = pl.DeviceIdType.MESH
F32, BF16 = jnp.float32, jnp.bfloat16
TRANSPOSED = (((0,), (0,)), ((), ()))

momentum_decay = 0.95
linear_coef = 3.4445
cubic_coef = -4.775
quintic_coef = 2.0315
norm_epsilon = 1e-07

DEVICES, CHIPS, CORES = 128, 64, 2
ROWS, FF = 16, 768
TILE = 256
CHUNKS = 4
GROUPS = 8
STORES = 4
CAP = 2
HALVES = 2
BLOCKS = CORES * HALVES


def displacement(step):
    n = lax.rem(step * 21, CHIPS)
    return lax.div(n, 16), lax.rem(lax.div(n, 4), 4), lax.rem(n, 4)


def kernel(
    g_hbm, m_hbm, table_hbm, fresh_hbm, update_hbm, log_hbm,
    gv, mv, rows, sent, gram, poly, total, rms_rows, table, log,
    load_sem, fresh_sem, send_sem, recv_sem, own_sem, back_send, back_recv, rms_send, rms_recv,
):
    y, o = lax.axis_index("dp"), lax.axis_index("owner")
    x, z, core = lax.div(o, 8), lax.rem(lax.div(o, 2), 4), lax.rem(o, 2)
    me = y * 32 + o
    sign = 1 - 2 * core

    def chip_at(step, direction):
        dy, dx, dz = displacement(step)
        ty = lax.rem(y + direction * dy + 4, 4)
        tx = lax.rem(x + direction * dx + 4, 4)
        tz = lax.rem(z + direction * dz + 4, 4)
        return ty, tx * 8 + tz * 2

    barrier = pltpu.get_barrier_semaphore()

    per = CHIPS // CHUNKS
    loads = []
    for phase in range(CORES):
        for k in range(CHUNKS):
            part = pl.ds(k * per, per)
            loads.append(
                (
                    pltpu.make_async_copy(
                        g_hbm.at[part, phase], gv.at[part, phase], load_sem.at[0, phase, k]
                    ),
                    pltpu.make_async_copy(
                        m_hbm.at[part, phase], mv.at[part, phase], load_sem.at[1, phase, k]
                    ),
                )
            )

    def load(phase):
        for pair in loads[phase * CHUNKS : (phase + 1) * CHUNKS]:
            for copy in pair:
                copy.start()

    load(0)

    for dy in range(4):
        ty = lax.rem(y + dy, 4)

        def greet(i, carry):
            pl.semaphore_signal(
                barrier, inc=1, device_id=(ty, lax.rem(o + i, 32)), device_id_type=MESH
            )
            return carry

        lax.fori_loop(0 if dy else 1, 32, greet, 0)

    load(1)
    table_copy = pltpu.make_async_copy(table_hbm, table, own_sem.at[2])
    table_copy.start()

    def effective(phase):
        for k in range(CHUNKS):
            for copy in loads[phase * CHUNKS + k]:
                copy.wait()

            def one(i, carry):
                grad = gv[i, phase].astype(F32)
                fresh = momentum_decay * mv[i, phase] + grad
                mv[i, phase] = fresh
                gv[i, phase] = (grad + momentum_decay * fresh).astype(BF16)
                return carry

            lax.fori_loop(k * per, (k + 1) * per, one, 0)
            part = pl.ds(k * per, per)
            pltpu.make_async_copy(
                mv.at[part, phase], fresh_hbm.at[part, phase], fresh_sem.at[phase, k]
            ).start()

    def forward(phase):
        mine = y * 16 + x * 4 + z

        @pl.when(core != phase)
        def _():
            pltpu.make_async_remote_copy(
                src_ref=gv.at[mine, phase],
                dst_ref=rows.at[core, 0],
                send_sem=send_sem,
                recv_sem=recv_sem.at[0],
                device_id=(y, x * 8 + z * 2 + phase),
                device_id_type=MESH,
            ).start()

        @pl.when(core == phase)
        def _():
            pltpu.make_async_copy(gv.at[mine, phase], rows.at[core, 0], own_sem.at[0]).start()

        def one(step, carry):
            ty, to = chip_at(step, sign)
            pltpu.make_async_remote_copy(
                src_ref=gv.at[ty * 16 + lax.div(to, 2), phase],
                dst_ref=rows.at[core, step],
                send_sem=send_sem,
                recv_sem=recv_sem.at[lax.div(step, CHIPS // GROUPS)],
                device_id=(ty, to + phase),
                device_id_type=MESH,
            ).start()
            return carry

        lax.fori_loop(1, CHIPS, one, 0)

    effective(0)
    pl.semaphore_wait(barrier, DEVICES - 1)
    forward(0)
    effective(1)
    forward(1)

    size = CHIPS // GROUPS
    total[...] = jnp.zeros_like(total)

    def accumulate(j):
        block = rows[:, pl.ds(j * size, size)].reshape(CORES * size * ROWS, FF)
        flipped = block.T
        for b in range(FF // TILE):
            n = TILE * (b + 1)
            total[0:n, TILE * b : n] += jnp.dot(
                flipped[0:n], block[:, TILE * b : n], preferred_element_type=F32
            )

    pltpu.make_async_copy(rows.at[0, 0], rows.at[0, 0], own_sem.at[0]).wait()
    remote = rows.at[0, pl.ds(0, CORES * size - 1)]
    pltpu.make_async_copy(remote, remote, recv_sem.at[0]).wait()
    accumulate(0)

    def arrive(j, carry):
        part = rows.at[:, pl.ds(j * size, size)]
        pltpu.make_async_copy(part, part, recv_sem.at[j]).wait()
        accumulate(j)
        return carry

    lax.fori_loop(1, GROUPS, arrive, 0)

    on_diagonal = lax.broadcasted_iota(jnp.int32, (TILE, TILE), 0) == lax.broadcasted_iota(
        jnp.int32, (TILE, TILE), 1
    )
    squares = jnp.zeros((1, 1), F32)
    for b in range(FF // TILE):
        s = slice(TILE * b, TILE * (b + 1))
        squares += jnp.sum(jnp.where(on_diagonal, total[s, s], 0.0), keepdims=True)
    inverse = 1.0 / (jnp.sqrt(squares) + norm_epsilon)

    def mirror(ref, b, upper):
        n = TILE * (b + 1)
        ref[0:n, TILE * b : n] = upper
        for a in range(b):
            ref[TILE * b : n, TILE * a : TILE * (a + 1)] = upper[TILE * a : TILE * (a + 1)].T

    for b in range(FF // TILE):
        n = TILE * (b + 1)
        mirror(gram, b, (total[0:n, TILE * b : n] * inverse * inverse).astype(BF16))

    def polynomial():
        for b in range(FF // TILE):
            n = TILE * (b + 1)
            square = jnp.dot(gram[0:n, :], gram[:, TILE * b : n], preferred_element_type=F32)
            upper = (
                cubic_coef * gram[0:n, TILE * b : n].astype(F32) + quintic_coef * square
            ).astype(BF16)
            mirror(poly, b, upper)

    span = CHIPS // HALVES

    def apply(current):
        return (
            linear_coef * current.astype(F32)
            + jnp.dot(current, poly[...], preferred_element_type=F32)
        ).astype(BF16)

    polynomial()

    def first(c, carry):
        start = (rows[c].reshape(CHIPS * ROWS, FF).astype(F32) * inverse).astype(BF16)
        rows[c] = apply(start).reshape(CHIPS, ROWS, FF)
        return carry

    lax.fori_loop(0, CORES, first, 0)

    whole = rows[...].reshape(DEVICES * ROWS, FF)
    for b in range(FF // TILE):
        n = TILE * (b + 1)
        mirror(
            gram,
            b,
            lax.dot_general(
                whole[:, 0:n], whole[:, TILE * b : n], TRANSPOSED, preferred_element_type=F32
            ).astype(BF16),
        )
    polynomial()

    full_rows = DEVICES * ROWS

    lane = lax.broadcasted_iota(jnp.int32, (1, DEVICES), 1)

    def send_back(step, c):
        ty, to = chip_at(step, 2 * c - 1)
        pltpu.make_async_remote_copy(
            src_ref=sent.at[c, step],
            dst_ref=update_hbm.at[me],
            send_sem=back_send,
            recv_sem=back_recv,
            device_id=(ty, to + c),
            device_id_type=MESH,
        ).start()

    def send_half(c, half):
        if half == 0:

            @pl.when(core == c)
            def _():
                pltpu.make_async_copy(sent.at[c, 0], update_hbm.at[me], own_sem.at[1]).start()

            @pl.when(core != c)
            def _():
                send_back(0, c)

        def one(step, carry):
            send_back(step, c)
            return carry

        lax.fori_loop(max(half * span, 1), (half + 1) * span, one, 0)

    def last(j, energy):
        c, half = lax.div(j, HALVES), lax.rem(j, HALVES)
        part = pl.ds(half * span, span)
        ortho = apply(rows[c, part].reshape(span * ROWS, FF)).astype(F32)
        sent[c, part] = (math.sqrt(full_rows) * ortho).astype(BF16).reshape(span, ROWS, FF)
        energy += jnp.sum((ortho * ortho).reshape(-1, 8, FF), axis=0)
        pl.when(j == 0)(lambda: send_half(0, 0))
        return energy

    energy = lax.fori_loop(0, BLOCKS, last, jnp.zeros((8, FF), F32))
    mean = jnp.sum(energy, keepdims=True) / (full_rows * FF)
    rms = math.sqrt(full_rows) * jnp.sqrt(mean)
    rms_rows[me] = jnp.where(lane == me, rms, 0.0)

    column, place = lax.div(me, 8), lax.rem(me, 8)
    mine_too = pl.ds(column * 8, 8)
    for i in range(1, 8):
        pltpu.make_async_remote_copy(
            src_ref=rms_rows.at[me],
            dst_ref=rms_rows.at[me],
            send_sem=rms_send.at[0],
            recv_sem=rms_recv.at[0],
            device_id=(y, x * 8 + lax.rem(place + i, 8)),
            device_id_type=MESH,
        ).start()

    def spread():
        seven = rms_rows.at[pl.ds(0, 7)]
        pltpu.make_async_copy(seven, seven, rms_recv.at[0]).wait()
        for i in range(1, 16):
            other = lax.rem(column + i, 16)
            pltpu.make_async_remote_copy(
                src_ref=rms_rows.at[mine_too],
                dst_ref=rms_rows.at[mine_too],
                send_sem=rms_send.at[1],
                recv_sem=rms_recv.at[1],
                device_id=(lax.div(other, 4), lax.rem(other, 4) * 8 + place),
                device_id_type=MESH,
            ).start()

    send_half(0, 1)

    @pl.when(core == 0)
    def _():
        send_half(1, 0)
        send_half(1, 1)
        spread()

    @pl.when(core == 1)
    def _():
        spread()
        send_half(1, 0)
        send_half(1, 1)

    others = pl.ds(0, DEVICES - 1)
    for stage, count in ((0, 7), (1, DEVICES - 8)):
        part = rms_rows.at[pl.ds(0, count)]
        pltpu.make_async_copy(part, part, rms_send.at[stage]).wait()
        if stage:
            pltpu.make_async_copy(part, part, rms_recv.at[stage]).wait()

    every = jnp.sum(rms_rows[...], axis=0)
    table_copy.wait()
    owned = table[...] == me
    low = jnp.min(jnp.where(owned, lane, DEVICES), keepdims=True)
    high = jnp.max(jnp.where(owned, lane, -1), keepdims=True)
    first_rms = jnp.sum(jnp.where(lane == low, every, 0.0), keepdims=True)
    second_rms = jnp.sum(jnp.where((lane == high) & (high > low), every, 0.0), keepdims=True)
    log[...] = jnp.where(lane == 0, first_rms, jnp.where(lane == 1, second_rms, 0.0))[:, :CAP]
    log_copy = pltpu.make_async_copy(log, log_hbm, own_sem.at[3])
    log_copy.start()

    for phase in range(CORES):
        for k in range(CHUNKS):
            part = pl.ds(k * per, per)
            pltpu.make_async_copy(
                mv.at[part, phase], fresh_hbm.at[part, phase], fresh_sem.at[phase, k]
            ).wait()
    pltpu.make_async_copy(update_hbm.at[others], update_hbm.at[others], send_sem).wait()
    pltpu.make_async_copy(update_hbm.at[others], update_hbm.at[others], back_send).wait()
    pltpu.make_async_copy(sent.at[0, 0], update_hbm.at[me], own_sem.at[1]).wait()
    pltpu.make_async_copy(update_hbm.at[others], update_hbm.at[others], back_recv).wait()
    log_copy.wait()


def store(fresh_ref, update_ref, log_ref, fresh_out, update_out, log_out, sem):
    per = DEVICES // STORES
    copies = [pltpu.make_async_copy(log_ref, log_out, sem.at[2, 0])]
    for k in range(STORES):
        part = pl.ds(k * per, per)
        copies.append(pltpu.make_async_copy(fresh_ref.at[part], fresh_out.at[part], sem.at[0, k]))
        copies.append(pltpu.make_async_copy(update_ref.at[part], update_out.at[part], sem.at[1, k]))
    for copy in copies:
        copy.start()
    for copy in copies:
        copy.wait()


def on_device(gradient, momentum, owner_table):
    paired = (CHIPS, CORES, ROWS, FF)
    anywhere = pl.BlockSpec(memory_space=pl.ANY)
    in_hbm = pl.BlockSpec(memory_space=pltpu.HBM)
    fresh, update, log = pl.pallas_call(
        kernel,
        out_shape=(
            jax.ShapeDtypeStruct(paired, F32),
            jax.ShapeDtypeStruct((DEVICES, ROWS, FF), BF16),
            jax.ShapeDtypeStruct((1, CAP), F32),
        ),
        in_specs=[in_hbm, in_hbm, in_hbm],
        out_specs=(anywhere, anywhere, anywhere),
        scratch_shapes=[
            pltpu.VMEM(paired, BF16),
            pltpu.VMEM(paired, F32),
            pltpu.VMEM((CORES, CHIPS, ROWS, FF), BF16),
            pltpu.VMEM((CORES, CHIPS, ROWS, FF), BF16),
            pltpu.VMEM((FF, FF), BF16),
            pltpu.VMEM((FF, FF), BF16),
            pltpu.VMEM((FF, FF), F32),
            pltpu.VMEM((DEVICES, 1, DEVICES), F32),
            pltpu.VMEM((1, DEVICES), jnp.int32),
            pltpu.VMEM((1, CAP), F32),
            pltpu.SemaphoreType.DMA((2, CORES, CHUNKS)),
            pltpu.SemaphoreType.DMA((CORES, CHUNKS)),
            pltpu.SemaphoreType.DMA,
            pltpu.SemaphoreType.DMA((GROUPS,)),
            pltpu.SemaphoreType.DMA((4,)),
            pltpu.SemaphoreType.DMA,
            pltpu.SemaphoreType.DMA,
            pltpu.SemaphoreType.DMA((2,)),
            pltpu.SemaphoreType.DMA((2,)),
        ],
        compiler_params=pltpu.CompilerParams(
            collective_id=0, has_side_effects=True, vmem_limit_bytes=40 * 2**20
        ),
        cost_estimate=pl.CostEstimate(
            flops=11 * 10**9, bytes_accessed=18 * 2**20, transcendentals=0
        ),
        name="orthogonalize",
    )(
        pltpu.with_memory_space_constraint(gradient.reshape(paired), pltpu.HBM),
        pltpu.with_memory_space_constraint(momentum.reshape(paired), pltpu.HBM),
        pltpu.with_memory_space_constraint(owner_table.reshape(1, DEVICES), pltpu.HBM),
    )
    return pl.pallas_call(
        store,
        out_shape=(
            jax.ShapeDtypeStruct(momentum.shape, F32),
            jax.ShapeDtypeStruct(update.shape, BF16),
            jax.ShapeDtypeStruct((1, CAP), F32),
        ),
        in_specs=[anywhere, anywhere, anywhere],
        out_specs=(in_hbm, in_hbm, in_hbm),
        scratch_shapes=[pltpu.SemaphoreType.DMA((3, STORES))],
        compiler_params=pltpu.CompilerParams(vmem_limit_bytes=2**20),
        name="store",
    )(fresh.reshape(momentum.shape), update, log)


def solution(mesh):
    split = P(None, AXES, None)
    return jax.shard_map(
        on_device,
        mesh=mesh,
        in_specs=(split, split, P()),
        out_specs=(split, split, P(AXES, None)),
        check_vma=False,
    )
```

```python
import math

import jax
import jax.numpy as jnp
from jax import lax
from jax.experimental import pallas as pl
from jax.experimental.pallas import tpu as pltpu
from jax.sharding import PartitionSpec as P

AXES = ("dp", "owner")
MESH = pl.DeviceIdType.MESH
F32, BF16 = jnp.float32, jnp.bfloat16
TRANSPOSED = (((0,), (0,)), ((), ()))

momentum_decay = 0.95
linear_coef = 3.4445
cubic_coef = -4.775
quintic_coef = 2.0315
norm_epsilon = 1e-07

DEVICES, CHIPS, CORES = 128, 64, 2
ROWS, FF = 16, 768
TILE = 256
CHUNKS = 4
GROUPS = 8
STORES = 4
CAP = 2
HALVES = 2
BLOCKS = CORES * HALVES


def displacement(step):
    n = lax.rem(step * 21, CHIPS)
    return lax.div(n, 16), lax.rem(lax.div(n, 4), 4), lax.rem(n, 4)


def kernel(
    g_hbm, m_hbm, table_hbm, fresh_hbm, update_hbm, log_hbm,
    gv, mv, rows, sent, gram, poly, total, rms_rows, table, log,
    load_sem, fresh_sem, send_sem, recv_sem, own_sem, back_send, back_recv, rms_send, rms_recv,
):
    y, o = lax.axis_index("dp"), lax.axis_index("owner")
    x, z, core = lax.div(o, 8), lax.rem(lax.div(o, 2), 4), lax.rem(o, 2)
    me = y * 32 + o
    sign = 1 - 2 * core

    def chip_at(step, direction):
        dy, dx, dz = displacement(step)
        ty = lax.rem(y + direction * dy + 4, 4)
        tx = lax.rem(x + direction * dx + 4, 4)
        tz = lax.rem(z + direction * dz + 4, 4)
        return ty, tx * 8 + tz * 2

    barrier = pltpu.get_barrier_semaphore()

    def greet(i, carry):
        t = lax.rem(me + 37 * i, DEVICES)
        pl.semaphore_signal(
            barrier, inc=1, device_id=(lax.div(t, 32), lax.rem(t, 32)), device_id_type=MESH
        )
        return carry

    lax.fori_loop(1, DEVICES, greet, 0)

    per = CHIPS // CHUNKS
    loads = []
    for phase in range(CORES):
        for k in range(CHUNKS):
            part = pl.ds(k * per, per)
            pair = (
                pltpu.make_async_copy(
                    g_hbm.at[part, phase], gv.at[part, phase], load_sem.at[0, phase, k]
                ),
                pltpu.make_async_copy(
                    m_hbm.at[part, phase], mv.at[part, phase], load_sem.at[1, phase, k]
                ),
            )
            for copy in pair:
                copy.start()
            loads.append(pair)

    table_copy = pltpu.make_async_copy(table_hbm, table, own_sem.at[2])
    table_copy.start()

    def effective(phase):
        for k in range(CHUNKS):
            for copy in loads[phase * CHUNKS + k]:
                copy.wait()

            def one(i, carry):
                grad = gv[i, phase].astype(F32)
                fresh = momentum_decay * mv[i, phase] + grad
                mv[i, phase] = fresh
                gv[i, phase] = (grad + momentum_decay * fresh).astype(BF16)
                return carry

            lax.fori_loop(k * per, (k + 1) * per, one, 0)
            part = pl.ds(k * per, per)
            pltpu.make_async_copy(
                mv.at[part, phase], fresh_hbm.at[part, phase], fresh_sem.at[phase, k]
            ).start()

    def forward(phase):
        mine = y * 16 + x * 4 + z

        @pl.when(core != phase)
        def _():
            pltpu.make_async_remote_copy(
                src_ref=gv.at[mine, phase],
                dst_ref=rows.at[core, 0],
                send_sem=send_sem,
                recv_sem=recv_sem.at[0],
                device_id=(y, x * 8 + z * 2 + phase),
                device_id_type=MESH,
            ).start()

        @pl.when(core == phase)
        def _():
            pltpu.make_async_copy(gv.at[mine, phase], rows.at[core, 0], own_sem.at[0]).start()

        def one(step, carry):
            ty, to = chip_at(step, sign)
            pltpu.make_async_remote_copy(
                src_ref=gv.at[ty * 16 + lax.div(to, 2), phase],
                dst_ref=rows.at[core, step],
                send_sem=send_sem,
                recv_sem=recv_sem.at[lax.div(step, CHIPS // GROUPS)],
                device_id=(ty, to + phase),
                device_id_type=MESH,
            ).start()
            return carry

        lax.fori_loop(1, CHIPS, one, 0)

    effective(0)
    pl.semaphore_wait(barrier, DEVICES - 1)
    forward(0)
    effective(1)
    forward(1)

    size = CHIPS // GROUPS
    total[...] = jnp.zeros_like(total)

    def accumulate(j):
        block = rows[:, pl.ds(j * size, size)].reshape(CORES * size * ROWS, FF)
        flipped = block.T
        for b in range(FF // TILE):
            n = TILE * (b + 1)
            total[0:n, TILE * b : n] += jnp.dot(
                flipped[0:n], block[:, TILE * b : n], preferred_element_type=F32
            )

    pltpu.make_async_copy(rows.at[0, 0], rows.at[0, 0], own_sem.at[0]).wait()
    remote = rows.at[0, pl.ds(0, CORES * size - 1)]
    pltpu.make_async_copy(remote, remote, recv_sem.at[0]).wait()
    accumulate(0)

    def arrive(j, carry):
        part = rows.at[:, pl.ds(j * size, size)]
        pltpu.make_async_copy(part, part, recv_sem.at[j]).wait()
        accumulate(j)
        return carry

    lax.fori_loop(1, GROUPS, arrive, 0)

    on_diagonal = lax.broadcasted_iota(jnp.int32, (TILE, TILE), 0) == lax.broadcasted_iota(
        jnp.int32, (TILE, TILE), 1
    )
    squares = jnp.zeros((1, 1), F32)
    for b in range(FF // TILE):
        s = slice(TILE * b, TILE * (b + 1))
        squares += jnp.sum(jnp.where(on_diagonal, total[s, s], 0.0), keepdims=True)
    inverse = 1.0 / (jnp.sqrt(squares) + norm_epsilon)

    def mirror(ref, b, upper):
        n = TILE * (b + 1)
        ref[0:n, TILE * b : n] = upper
        for a in range(b):
            ref[TILE * b : n, TILE * a : TILE * (a + 1)] = upper[TILE * a : TILE * (a + 1)].T

    for b in range(FF // TILE):
        n = TILE * (b + 1)
        mirror(gram, b, (total[0:n, TILE * b : n] * inverse * inverse).astype(BF16))

    def polynomial():
        for b in range(FF // TILE):
            n = TILE * (b + 1)
            square = jnp.dot(gram[0:n, :], gram[:, TILE * b : n], preferred_element_type=F32)
            upper = (
                cubic_coef * gram[0:n, TILE * b : n].astype(F32) + quintic_coef * square
            ).astype(BF16)
            mirror(poly, b, upper)

    span = CHIPS // HALVES

    def apply(current):
        return (
            linear_coef * current.astype(F32)
            + jnp.dot(current, poly[...], preferred_element_type=F32)
        ).astype(BF16)

    polynomial()

    def first(c, carry):
        start = (rows[c].reshape(CHIPS * ROWS, FF).astype(F32) * inverse).astype(BF16)
        rows[c] = apply(start).reshape(CHIPS, ROWS, FF)
        return carry

    lax.fori_loop(0, CORES, first, 0)

    whole = rows[...].reshape(DEVICES * ROWS, FF)
    for b in range(FF // TILE):
        n = TILE * (b + 1)
        mirror(
            gram,
            b,
            lax.dot_general(
                whole[:, 0:n], whole[:, TILE * b : n], TRANSPOSED, preferred_element_type=F32
            ).astype(BF16),
        )
    polynomial()

    full_rows = DEVICES * ROWS

    lane = lax.broadcasted_iota(jnp.int32, (1, DEVICES), 1)

    def send_back(step, c):
        ty, to = chip_at(step, 2 * c - 1)
        pltpu.make_async_remote_copy(
            src_ref=sent.at[c, step],
            dst_ref=update_hbm.at[me],
            send_sem=back_send,
            recv_sem=back_recv,
            device_id=(ty, to + c),
            device_id_type=MESH,
        ).start()

    def send_half(c, half):
        if half == 0:

            @pl.when(core == c)
            def _():
                pltpu.make_async_copy(sent.at[c, 0], update_hbm.at[me], own_sem.at[1]).start()

            @pl.when(core != c)
            def _():
                send_back(0, c)

        def one(step, carry):
            send_back(step, c)
            return carry

        lax.fori_loop(max(half * span, 1), (half + 1) * span, one, 0)

    def last(j, energy):
        c, half = lax.div(j, HALVES), lax.rem(j, HALVES)
        part = pl.ds(half * span, span)
        ortho = apply(rows[c, part].reshape(span * ROWS, FF)).astype(F32)
        sent[c, part] = (math.sqrt(full_rows) * ortho).astype(BF16).reshape(span, ROWS, FF)
        energy += jnp.sum((ortho * ortho).reshape(-1, 8, FF), axis=0)
        pl.when(j == 0)(lambda: send_half(0, 0))
        return energy

    energy = lax.fori_loop(0, BLOCKS, last, jnp.zeros((8, FF), F32))
    mean = jnp.sum(energy, keepdims=True) / (full_rows * FF)
    rms = math.sqrt(full_rows) * jnp.sqrt(mean)
    rms_rows[me] = jnp.where(lane == me, rms, 0.0)

    column, place = lax.div(me, 8), lax.rem(me, 8)
    mine_too = pl.ds(column * 8, 8)
    for i in range(1, 8):
        pltpu.make_async_remote_copy(
            src_ref=rms_rows.at[me],
            dst_ref=rms_rows.at[me],
            send_sem=rms_send.at[0],
            recv_sem=rms_recv.at[0],
            device_id=(y, x * 8 + lax.rem(place + i, 8)),
            device_id_type=MESH,
        ).start()

    def spread():
        seven = rms_rows.at[pl.ds(0, 7)]
        pltpu.make_async_copy(seven, seven, rms_recv.at[0]).wait()
        for i in range(1, 16):
            other = lax.rem(column + i, 16)
            pltpu.make_async_remote_copy(
                src_ref=rms_rows.at[mine_too],
                dst_ref=rms_rows.at[mine_too],
                send_sem=rms_send.at[1],
                recv_sem=rms_recv.at[1],
                device_id=(lax.div(other, 4), lax.rem(other, 4) * 8 + place),
                device_id_type=MESH,
            ).start()

    send_half(0, 1)

    @pl.when(core == 0)
    def _():
        send_half(1, 0)
        send_half(1, 1)
        spread()

    @pl.when(core == 1)
    def _():
        spread()
        send_half(1, 0)
        send_half(1, 1)

    others = pl.ds(0, DEVICES - 1)
    for stage, count in ((0, 7), (1, DEVICES - 8)):
        part = rms_rows.at[pl.ds(0, count)]
        pltpu.make_async_copy(part, part, rms_send.at[stage]).wait()
        if stage:
            pltpu.make_async_copy(part, part, rms_recv.at[stage]).wait()

    every = jnp.sum(rms_rows[...], axis=0)
    table_copy.wait()
    owned = table[...] == me
    low = jnp.min(jnp.where(owned, lane, DEVICES), keepdims=True)
    high = jnp.max(jnp.where(owned, lane, -1), keepdims=True)
    first_rms = jnp.sum(jnp.where(lane == low, every, 0.0), keepdims=True)
    second_rms = jnp.sum(jnp.where((lane == high) & (high > low), every, 0.0), keepdims=True)
    log[...] = jnp.where(lane == 0, first_rms, jnp.where(lane == 1, second_rms, 0.0))[:, :CAP]
    log_copy = pltpu.make_async_copy(log, log_hbm, own_sem.at[3])
    log_copy.start()

    for phase in range(CORES):
        for k in range(CHUNKS):
            part = pl.ds(k * per, per)
            pltpu.make_async_copy(
                mv.at[part, phase], fresh_hbm.at[part, phase], fresh_sem.at[phase, k]
            ).wait()
    pltpu.make_async_copy(update_hbm.at[others], update_hbm.at[others], send_sem).wait()
    pltpu.make_async_copy(update_hbm.at[others], update_hbm.at[others], back_send).wait()
    pltpu.make_async_copy(sent.at[0, 0], update_hbm.at[me], own_sem.at[1]).wait()
    pltpu.make_async_copy(update_hbm.at[others], update_hbm.at[others], back_recv).wait()
    log_copy.wait()


def store(fresh_ref, update_ref, log_ref, fresh_out, update_out, log_out, sem):
    per = DEVICES // STORES
    copies = [pltpu.make_async_copy(log_ref, log_out, sem.at[2, 0])]
    for k in range(STORES):
        part = pl.ds(k * per, per)
        copies.append(pltpu.make_async_copy(fresh_ref.at[part], fresh_out.at[part], sem.at[0, k]))
        copies.append(pltpu.make_async_copy(update_ref.at[part], update_out.at[part], sem.at[1, k]))
    for copy in copies:
        copy.start()
    for copy in copies:
        copy.wait()


def on_device(gradient, momentum, owner_table):
    paired = (CHIPS, CORES, ROWS, FF)
    anywhere = pl.BlockSpec(memory_space=pl.ANY)
    in_hbm = pl.BlockSpec(memory_space=pltpu.HBM)
    fresh, update, log = pl.pallas_call(
        kernel,
        out_shape=(
            jax.ShapeDtypeStruct(paired, F32),
            jax.ShapeDtypeStruct((DEVICES, ROWS, FF), BF16),
            jax.ShapeDtypeStruct((1, CAP), F32),
        ),
        in_specs=[in_hbm, in_hbm, in_hbm],
        out_specs=(anywhere, anywhere, anywhere),
        scratch_shapes=[
            pltpu.VMEM(paired, BF16),
            pltpu.VMEM(paired, F32),
            pltpu.VMEM((CORES, CHIPS, ROWS, FF), BF16),
            pltpu.VMEM((CORES, CHIPS, ROWS, FF), BF16),
            pltpu.VMEM((FF, FF), BF16),
            pltpu.VMEM((FF, FF), BF16),
            pltpu.VMEM((FF, FF), F32),
            pltpu.VMEM((DEVICES, 1, DEVICES), F32),
            pltpu.VMEM((1, DEVICES), jnp.int32),
            pltpu.VMEM((1, CAP), F32),
            pltpu.SemaphoreType.DMA((2, CORES, CHUNKS)),
            pltpu.SemaphoreType.DMA((CORES, CHUNKS)),
            pltpu.SemaphoreType.DMA,
            pltpu.SemaphoreType.DMA((GROUPS,)),
            pltpu.SemaphoreType.DMA((4,)),
            pltpu.SemaphoreType.DMA,
            pltpu.SemaphoreType.DMA,
            pltpu.SemaphoreType.DMA((2,)),
            pltpu.SemaphoreType.DMA((2,)),
        ],
        compiler_params=pltpu.CompilerParams(
            collective_id=0, has_side_effects=True, vmem_limit_bytes=40 * 2**20
        ),
        cost_estimate=pl.CostEstimate(
            flops=11 * 10**9, bytes_accessed=18 * 2**20, transcendentals=0
        ),
        name="orthogonalize",
    )(
        pltpu.with_memory_space_constraint(gradient.reshape(paired), pltpu.HBM),
        pltpu.with_memory_space_constraint(momentum.reshape(paired), pltpu.HBM),
        pltpu.with_memory_space_constraint(owner_table.reshape(1, DEVICES), pltpu.HBM),
    )
    return pl.pallas_call(
        store,
        out_shape=(
            jax.ShapeDtypeStruct(momentum.shape, F32),
            jax.ShapeDtypeStruct(update.shape, BF16),
            jax.ShapeDtypeStruct((1, CAP), F32),
        ),
        in_specs=[anywhere, anywhere, anywhere],
        out_specs=(in_hbm, in_hbm, in_hbm),
        scratch_shapes=[pltpu.SemaphoreType.DMA((3, STORES))],
        compiler_params=pltpu.CompilerParams(vmem_limit_bytes=2**20),
        name="store",
    )(fresh.reshape(momentum.shape), update, log)


def solution(mesh):
    split = P(None, AXES, None)
    return jax.shard_map(
        on_device,
        mesh=mesh,
        in_specs=(split, split, P()),
        out_specs=(split, split, P(AXES, None)),
        check_vma=False,
    )
```
